128 devices in a mesh: obs: 8 (over z, core), src: 16 (over y, x).
Axes of the slice: x: 4, y: 4, z: 4, core: 2. Of those that a mesh axis runs over, the one named last changes fastest.
Arguments:
- history: bfloat16 [3, 256, 64, 1536], P(None, ('obs', 'src')), may hold values from -6 to 6
- incident: bfloat16 [5, 256, 64, 1536], P(None, ('obs', 'src')), may hold values from -6 to 6
- proj_basis: bfloat16 [256, 64, 1536], P(('obs', 'src')), may hold values from -0.15625 to 0.15625
- expand_basis: bfloat16 [256, 64, 1536], P(('obs', 'src')), may hold values from -0.75 to 0.75
- near_inverse: bfloat16 [256, 1536, 1536], P(('obs', 'src')), may hold values from -0.15625 to 0.15625
- couplings: bfloat16 [2, 16384, 8, 16, 128], P(None, 'obs', None, 'src'), may hold values from -0.046875 to 0.046875
- lags: int32 [256, 8, 16, 2], P('obs', None, 'src'), may hold values from 0 to 2, as said below
Outputs:
- currents: bfloat16 [5, 256, 64, 1536], P(None, ('obs', 'src'))
The draws below stay inside these ranges and needn't reach their ends.
Inputs may be any that keep to these rules, and one draw needn't show every extreme that they name: lags[j, o, s, k] is the lag from source cluster j to observer cluster (o * 16 + s) * 2 + k. Entries are 0, 1 or 2, and the entry of every cluster with itself is 0.
All inputs are finite; a program needn't handle non-finite values.
Results may differ from the reference program's by a relative error of at most 0.025.
Values may be sent and summed in bfloat16 or wider, within the bound.
No kernel may reach another device: no remote copies, remote signals or barrier semaphores. Data moves between devices by JAX's collectives and lax.ppermute only.
A program may use at most 192 MiB of HBM per device.

```python
import math
import jax
import jax.numpy as jnp
from jax import lax

CL_DEV = 2
B = 1536
R = 64
E = 64
STEPS = 5
TAPS = 2
HIST = 3
C = 256
N_OBS = 8
N_SRC = 16


def draw_lags(key, part):
    shape = (C, N_OBS, N_SRC, CL_DEV)
    raw_value = jax.random.randint(key, shape, 0, 8)
    lag_value = jnp.where(raw_value == 0, 0, jnp.where(raw_value <= 4, 1, 2))
    source = lax.broadcasted_iota(jnp.int32, shape, 0)
    observer = (lax.broadcasted_iota(jnp.int32, shape, 1) * N_SRC + lax.broadcasted_iota(jnp.int32, shape, 2)) * CL_DEV + lax.broadcasted_iota(jnp.int32, shape, 3)
    return jnp.where(source == observer, 0, lag_value).astype(jnp.int32)


def strengthened(array, stream_key, source, target, parts, factor):
    owner, partner = [(jnp.arange(array.shape[axis_at]) // (array.shape[axis_at] // parts)).reshape([-1 if axis == axis_at else 1 for axis in range(array.ndim)]) for axis_at in (source, target)]
    chosen = jax.random.permutation(stream_key, parts)[partner]
    strong = (owner == chosen) | (owner == (partner + parts // 2) % parts)
    return jnp.where(strong, factor * array, array)


def block_levels(rng, dims, shards, low, top_value):
    def one(position, blocks):
        draws = jax.random.uniform(jax.random.fold_in(jax.random.fold_in(rng, 6), position), (blocks,), jnp.float32, low / len(shards), top_value / len(shards))
        return jnp.repeat(jnp.exp(draws), dims[position] // blocks).reshape((-1,) + (1,) * (len(dims) - position - 1))

    factor_of = one(*shards[0])
    for cut in shards[1:]:
        factor_of = factor_of * one(*cut)
    return factor_of


def bell_draw(own_key, shape, spread, most, shards=(), kind=jnp.bfloat16):
    drawn = jax.random.normal(own_key, shape, jnp.float32) * spread
    if len(shards) > 0:
        drawn = block_levels(own_key, shape, shards, -0.22, 0.18) * drawn
    return jnp.clip(drawn, min=-most, max=most).astype(kind)


def heavy_noise(key, shape, scale, limit, shards, heavy, held_as=jnp.bfloat16):
    drawn = scale * jax.random.normal(key, shape, jnp.float32)
    if shards:
        drawn = drawn * block_levels(key, shape, shards, -0.22, 0.18)
    return jnp.clip(strengthened(drawn, jax.random.fold_in(key, 3), *heavy), -limit, limit).astype(held_as)


def setup_inputs(seed: int = 0) -> dict:
    seeds = jax.random.split(jax.random.key(seed), 8)
    history = bell_draw(seeds[0], (HIST, C, E, B), 1.0, 6.0, ((1, 128),))
    incident = bell_draw(seeds[1], (STEPS, C, E, B), 1.0, 6.0, ((1, 128),))
    proj_basis = bell_draw(seeds[2], (C, R, B), B ** -0.5, 0.15625, ((0, 128),))
    expand_basis = bell_draw(seeds[3], (C, R, B), R ** -0.5, 0.75, ((0, 128),))
    near_inverse = bell_draw(seeds[4], (C, B, B), B ** -0.5, 0.15625, ((0, 128),))
    couplings = heavy_noise(seeds[5], (TAPS, C * R, N_OBS, N_SRC, CL_DEV * R), (2 * C * R) ** -0.5, 0.046875, ((1, 8), (3, 16)), (1, 2, 8, 2.0))
    lags = draw_lags(jax.random.fold_in(seeds[7], 71), 0)
    return dict(history=history, incident=incident, proj_basis=proj_basis, expand_basis=expand_basis, near_inverse=near_inverse, couplings=couplings, lags=lags)


def project(current, proj_basis):
    projected = jnp.einsum('ceb,crb->ecr', current.astype(jnp.float32), proj_basis.astype(jnp.float32), precision=lax.Precision.HIGHEST)
    return projected.astype(jnp.bfloat16).reshape(E, C * R)


def far_sum(stacked, kernel, lag_pairs):
    group_size = math.gcd(C, 16)
    block_count = C // group_size

    def one_block(block_index):
        start = (block_index * group_size).astype(jnp.int32)
        block_kernel = lax.dynamic_slice_in_dim(kernel, (start * R).astype(jnp.int32), group_size * R, 2)
        block_kernel = block_kernel.reshape(TAPS, C, R, group_size, R)
        block_lags = lax.dynamic_slice_in_dim(lag_pairs, start, group_size, 1)
        total = jnp.zeros((E, group_size * R), jnp.float32)
        for delay in range(1, HIST + 1):
            combined = jnp.zeros((C, R, group_size, R), jnp.bfloat16)
            for tap_index in range(TAPS):
                if delay - tap_index >= 1:
                    chosen = (block_lags == delay - tap_index)[:, None, :, None]
                    combined = jnp.where(chosen, block_kernel[tap_index], combined)
            total = total + jnp.dot(stacked[delay - 1], combined.reshape(C * R, group_size * R).astype(jnp.float32), precision=lax.Precision.HIGHEST)
        return total

    blocks = lax.map(one_block, jnp.arange(block_count, dtype=jnp.int32))
    return jnp.transpose(blocks, (1, 0, 2)).reshape(E, C * R)


def reference(history, incident, proj_basis, expand_basis, near_inverse, couplings, lags):
    kernel = couplings.reshape(TAPS, C * R, C * R)
    lag_pairs = lags.reshape(C, C)
    past = [project(history[slot_index], proj_basis) for slot_index in range(HIST)]
    results = []
    for step in range(STEPS):
        stacked = jnp.stack([past[len(past) - delay] for delay in range(1, HIST + 1)]).astype(jnp.float32)
        field = far_sum(stacked, kernel, lag_pairs).astype(jnp.bfloat16).reshape(E, C, R)
        far_field = jnp.einsum('ecr,crb->ceb', field.astype(jnp.float32), expand_basis.astype(jnp.float32), precision=lax.Precision.HIGHEST)
        residual_field = (incident[step].astype(jnp.float32) - far_field).astype(jnp.bfloat16)

        def near_apply(pair):
            return jnp.dot(pair[0].astype(jnp.float32), pair[1].astype(jnp.float32), precision=lax.Precision.HIGHEST)

        current = lax.map(near_apply, (residual_field, near_inverse)).astype(jnp.bfloat16)
        results.append(current)
        past.append(project(current, proj_basis))
    return jnp.stack(results)
```

```python
import jax
import jax.numpy as jnp
from jax import lax
from jax.experimental import pallas as pl
from jax.experimental.pallas import tpu as pltpu
from jax.sharding import PartitionSpec as P

STEPS = 5
HIST = 3
MIB = 1024 * 1024
BF16 = jnp.bfloat16
F32 = jnp.float32
VMEM_SPEC = pl.BlockSpec(memory_space=pltpu.VMEM)


def nt_dot(left, right):
    return lax.dot_general(left, right, (((1,), (1,)), ((), ())), preferred_element_type=F32)


def params(limit, **more):
    return pltpu.CompilerParams(vmem_limit_bytes=limit * MIB, **more)


def cost(flops, touched):
    return pl.CostEstimate(flops=int(flops), bytes_accessed=int(touched), transcendentals=0)


def history_kernel(history_ref, proj_ref, out_ref):
    slots, clusters, excite, unknowns = history_ref.shape
    parts = []
    for c in range(clusters):
        left = jnp.concatenate([history_ref[h, c] for h in range(slots)], axis=0)
        parts.append(nt_dot(left, proj_ref[c]))
    both = jnp.concatenate(parts, axis=1).astype(BF16)
    for s in range(out_ref.shape[0]):
        for h in range(slots):
            out_ref[s, h] = both[h * excite:(h + 1) * excite]


def project_history(history, proj_basis, copies):
    slots, clusters, excite, unknowns = history.shape
    rank = proj_basis.shape[1]
    return pl.pallas_call(
        history_kernel,
        out_shape=jax.ShapeDtypeStruct((copies, slots, excite, clusters * rank), BF16),
        in_specs=[VMEM_SPEC] * 2,
        out_specs=VMEM_SPEC,
        compiler_params=params(16),
        name="project_history",
    )(history, proj_basis)


def near_kernel(incident_ref, expand_ref, near_ref, proj_ref,
                incoming_ref, expanded_ref, start_ref, transfer_ref, acc_ref):
    c, n = pl.program_id(0), pl.program_id(1)
    steps, _, excite, unknowns = incident_ref.shape
    rank = expand_ref.shape[1]
    left = jnp.concatenate([incident_ref[t, 0] for t in range(steps)] + [expand_ref[0]], axis=0)
    product = jnp.dot(left, near_ref[0], preferred_element_type=F32).astype(BF16)
    for t in range(steps):
        incoming_ref[t, 0] = product[t * excite:(t + 1) * excite]
    expanded_ref[0] = product[steps * excite:]
    small = nt_dot(product, proj_ref[0])

    @pl.when(n == 0)
    def _():
        acc_ref[c] = small

    @pl.when(n > 0)
    def _():
        acc_ref[c] += small

    @pl.when((c == 1) & (n == pl.num_programs(1) - 1))
    def _():
        for t in range(steps):
            rows = slice(t * excite, (t + 1) * excite)
            start_ref[t] = jnp.concatenate([acc_ref[0, rows], acc_ref[1, rows]], axis=1)
        tail = slice(steps * excite, steps * excite + rank)
        zero = jnp.zeros((rank, rank), F32)
        full = jnp.concatenate([
            jnp.concatenate([acc_ref[0, tail], zero], axis=1),
            jnp.concatenate([zero, acc_ref[1, tail]], axis=1),
        ], axis=0)
        high = full.astype(BF16)
        low = (full - high.astype(F32)).astype(BF16)
        transfer_ref[...] = jnp.concatenate([high, low], axis=0)


def prepare_near(incident, expand_basis, near_inverse, proj_basis, tile=512):
    steps, clusters, excite, unknowns = incident.shape
    rank = proj_basis.shape[1]
    rows = steps * excite + rank
    return pl.pallas_call(
        near_kernel,
        grid=(clusters, unknowns // tile),
        out_shape=(
            jax.ShapeDtypeStruct((steps, clusters, excite, unknowns), BF16),
            jax.ShapeDtypeStruct((clusters, rank, unknowns), BF16),
            jax.ShapeDtypeStruct((steps, excite, clusters * rank), F32),
            jax.ShapeDtypeStruct((2 * clusters * rank, clusters * rank), BF16),
        ),
        in_specs=[
            pl.BlockSpec((steps, 1, excite, unknowns), lambda c, n: (0, c, 0, 0)),
            pl.BlockSpec((1, rank, unknowns), lambda c, n: (c, 0, 0)),
            pl.BlockSpec((1, unknowns, tile), lambda c, n: (c, 0, n)),
            pl.BlockSpec((1, rank, tile), lambda c, n: (c, 0, n)),
        ],
        out_specs=(
            pl.BlockSpec((steps, 1, excite, tile), lambda c, n: (0, c, 0, n)),
            pl.BlockSpec((1, rank, tile), lambda c, n: (c, 0, n)),
            pl.BlockSpec((steps, excite, clusters * rank), lambda c, n: (0, 0, 0)),
            pl.BlockSpec((2 * clusters * rank, clusters * rank), lambda c, n: (0, 0)),
        ),
        scratch_shapes=[pltpu.VMEM((clusters, rows, rank), F32)],
        compiler_params=params(24),
        cost_estimate=cost(2 * clusters * rows * unknowns * (unknowns + rank), 2 * clusters * unknowns * unknowns),
        name="prepare_near",
    )(incident, expand_basis, near_inverse, proj_basis)


def first_kernel(gathered_ref, couplings_ref, lags_ref,
                 w1_ref, w2_ref, w3_ref, field_ref, base_ref, perm_ref, acc_ref):
    i = pl.program_id(0)
    blocks = lags_ref.shape[1] // 128
    rows_in = 256
    group = rows_in // blocks
    rank = 64
    clusters_here = w1_ref.shape[0] // rank
    excite = gathered_ref.shape[2]

    @pl.when(i == 0)
    def _():
        to = lax.broadcasted_iota(jnp.int32, (rows_in, rows_in), 0)
        source = lax.broadcasted_iota(jnp.int32, (rows_in, rows_in), 1)
        wanted = (to % group) * blocks + to // group
        perm_ref[...] = jnp.where(source == wanted, 1.0, 0.0).astype(BF16)
        acc_ref[...] = jnp.zeros_like(acc_ref)

    perm = perm_ref[...]

    @pl.loop(0, clusters_here)
    def _(j):
        lag = lags_ref[pl.ds(i * clusters_here + j, 1), :]
        masks = []
        for wanted in (1.0, 2.0):
            row = jnp.where(lag == wanted, 1.0, 0.0)
            masks.append([
                jnp.broadcast_to(row[:, o * 128:(o + 1) * 128], (group, 128)).astype(BF16)
                for o in range(blocks)
            ])
        for g in range(rank // group):
            at = pl.multiple_of(j * (rank * blocks) + g * rows_in, rows_in)
            pair = jnp.concatenate(
                [couplings_ref[p, pl.ds(at, rows_in), :] for p in range(2)], axis=1)
            sorted_pair = jnp.dot(perm, pair, preferred_element_type=F32).astype(BF16)
            out = pl.ds(pl.multiple_of(j * rank + g * group, group), group)
            for o in range(blocks):
                k0 = sorted_pair[o * group:(o + 1) * group, :128]
                k1 = sorted_pair[o * group:(o + 1) * group, 128:]
                m1, m2 = masks[0][o], masks[1][o]
                lanes = slice(o * 128, (o + 1) * 128)
                w1_ref[out, lanes] = k0 * m1
                w2_ref[out, lanes] = k0 * m2 + k1 * m1
                w3_ref[out, lanes] = k1 * m2

    def left(h):
        return jnp.concatenate([gathered_ref[0, h], gathered_ref[1, h]], axis=1)

    old, middle, new = left(0), left(1), left(2)
    one = jnp.dot(new, w1_ref[...], preferred_element_type=F32)
    two = jnp.dot(jnp.concatenate([middle, new], axis=0), w2_ref[...], preferred_element_type=F32)
    three = jnp.dot(jnp.concatenate([old, middle, new], axis=0), w3_ref[...], preferred_element_type=F32)
    acc_ref[0] += one + two[:excite] + three[:excite]
    acc_ref[1] += two[excite:] + three[excite:2 * excite]
    acc_ref[2] += three[2 * excite:]

    @pl.when(i == pl.num_programs(0) - 1)
    def _():
        for o in range(blocks):
            field_ref[o] = acc_ref[0, :, o * 128:(o + 1) * 128].astype(BF16)
        base_ref[0] = acc_ref[1]
        base_ref[1] = acc_ref[2]


def first_step(gathered, couplings, lag_rows):
    senders, slots, excite, width = gathered.shape
    clusters, columns = lag_rows.shape
    rows = senders * width
    blocks = columns // 128
    steps = 8
    part = rows // steps
    matrix = jax.ShapeDtypeStruct((rows, columns), BF16)
    return pl.pallas_call(
        first_kernel,
        grid=(steps,),
        out_shape=(
            matrix, matrix, matrix,
            jax.ShapeDtypeStruct((blocks, excite, 128), BF16),
            jax.ShapeDtypeStruct((2, excite, columns), F32),
        ),
        in_specs=[
            pl.BlockSpec((senders // steps, slots, excite, width), lambda i: (i, 0, 0, 0)),
            pl.BlockSpec((2, part * blocks, 128), lambda i: (0, i, 0)),
            pl.BlockSpec((clusters, columns), lambda i: (0, 0)),
        ],
        out_specs=(
            pl.BlockSpec((part, columns), lambda i: (i, 0)),
            pl.BlockSpec((part, columns), lambda i: (i, 0)),
            pl.BlockSpec((part, columns), lambda i: (i, 0)),
            pl.BlockSpec((blocks, excite, 128), lambda i: (0, 0, 0)),
            pl.BlockSpec((2, excite, columns), lambda i: (0, 0, 0)),
        ),
        scratch_shapes=[
            pltpu.VMEM((256, 256), BF16),
            pltpu.VMEM((3, excite, columns), F32),
        ],
        compiler_params=params(24),
        cost_estimate=cost(2 * 6 * excite * rows * columns, 10 * rows * columns),
        name="first_step",
    )(gathered, couplings, lag_rows)


def wide(gathered_ref):
    return jnp.concatenate([gathered_ref[s] for s in range(gathered_ref.shape[0])], axis=1)


def send_field(field_ref, total):
    for o in range(field_ref.shape[0]):
        field_ref[o] = total[:, o * 128:(o + 1) * 128].astype(BF16)


def step1_kernel(q0_ref, base_ref, w1_ref, field_ref):
    send_field(field_ref, base_ref[0] + jnp.dot(wide(q0_ref), w1_ref[...], preferred_element_type=F32))


def step2_kernel(q0_ref, q1_ref, base_ref, w1_ref, w2_ref, field_ref, next_ref):
    excite = base_ref.shape[1]
    one, zero = wide(q1_ref), wide(q0_ref)
    two = jnp.dot(jnp.concatenate([zero, one], axis=0), w2_ref[...], preferred_element_type=F32)
    send_field(field_ref, base_ref[1] + two[:excite] + jnp.dot(one, w1_ref[...], preferred_element_type=F32))
    next_ref[...] = two[excite:]


def step3_kernel(q0_ref, q1_ref, q2_ref, base_ref, w1_ref, w3_ref, field_ref, next_ref):
    excite = base_ref.shape[0]
    three = jnp.dot(jnp.concatenate([wide(q0_ref), wide(q1_ref)], axis=0), w3_ref[...], preferred_element_type=F32)
    send_field(field_ref, base_ref[...] + three[:excite]
               + jnp.dot(wide(q2_ref), w1_ref[...], preferred_element_type=F32))
    next_ref[...] = three[excite:]


def step4_kernel(q2_ref, q3_ref, base_ref, w1_ref, w2_ref, field_ref):
    send_field(field_ref, base_ref[...]
               + jnp.dot(wide(q2_ref), w2_ref[...], preferred_element_type=F32)
               + jnp.dot(wide(q3_ref), w1_ref[...], preferred_element_type=F32))


def couple(kernel, name, blocks, with_next, *arrays):
    excite, width = arrays[0].shape[1:]
    shapes = [jax.ShapeDtypeStruct((blocks, excite, width), BF16)]
    if with_next:
        shapes.append(jax.ShapeDtypeStruct((excite, blocks * width), F32))
    got = pl.pallas_call(
        kernel,
        out_shape=shapes,
        in_specs=[VMEM_SPEC] * len(arrays),
        out_specs=[VMEM_SPEC] * len(shapes),
        compiler_params=params(24),
        name=name,
    )(*arrays)
    return got if with_next else got[0]


def project_kernel(parts_ref, start_ref, transfer_ref, field_ref, out_ref):
    total = parts_ref[0].astype(F32)
    for o in range(1, parts_ref.shape[0]):
        total = total + parts_ref[o].astype(F32)
    field = total.astype(BF16)
    field_ref[...] = field
    q = start_ref[0] - jnp.dot(
        jnp.concatenate([field, field], axis=1), transfer_ref[...], preferred_element_type=F32)
    q = q.astype(BF16)
    for s in range(out_ref.shape[0]):
        out_ref[s] = q


def project_step(parts, start, transfer, copies, step):
    blocks, excite, width = parts.shape
    return pl.pallas_call(
        project_kernel,
        grid=(1,),
        out_shape=(
            jax.ShapeDtypeStruct((excite, width), BF16),
            jax.ShapeDtypeStruct((copies, excite, width), BF16),
        ),
        in_specs=[
            pl.BlockSpec(parts.shape, lambda i: (0, 0, 0)),
            pl.BlockSpec((1, excite, width), lambda i: (step, 0, 0)),
            pl.BlockSpec(transfer.shape, lambda i: (0, 0)),
        ],
        out_specs=(
            pl.BlockSpec((excite, width), lambda i: (0, 0)),
            pl.BlockSpec((copies, excite, width), lambda i: (0, 0, 0)),
        ),
        compiler_params=params(8),
        name="project_step",
    )(parts, start, transfer)


def currents_kernel(incoming_ref, expanded_ref, parts_ref, f0_ref, f1_ref, f2_ref, f3_ref, out_ref):
    total = parts_ref[0].astype(F32)
    for o in range(1, parts_ref.shape[0]):
        total = total + parts_ref[o].astype(F32)
    fields = [f0_ref[...], f1_ref[...], f2_ref[...], f3_ref[...], total.astype(BF16)]
    excite = out_ref.shape[2]
    rank = expanded_ref.shape[1]
    for c in range(out_ref.shape[1]):
        left = jnp.concatenate([f[:, c * rank:(c + 1) * rank] for f in fields], axis=0)
        far = jnp.dot(left, expanded_ref[c], preferred_element_type=F32)
        for t in range(out_ref.shape[0]):
            out_ref[t, c] = (incoming_ref[t, c].astype(F32) - far[t * excite:(t + 1) * excite]).astype(BF16)


def final_currents(incoming, expanded, parts, fields, tile=512):
    steps, clusters, excite, unknowns = incoming.shape
    rank = expanded.shape[1]
    small = pl.BlockSpec(fields[0].shape, lambda n: (0, 0))
    return pl.pallas_call(
        currents_kernel,
        grid=(unknowns // tile,),
        out_shape=jax.ShapeDtypeStruct(incoming.shape, BF16),
        in_specs=[
            pl.BlockSpec((steps, clusters, excite, tile), lambda n: (0, 0, 0, n)),
            pl.BlockSpec((clusters, rank, tile), lambda n: (0, 0, n)),
            pl.BlockSpec(parts.shape, lambda n: (0, 0, 0)),
        ] + [small] * len(fields),
        out_specs=pl.BlockSpec((steps, clusters, excite, tile), lambda n: (0, 0, 0, n)),
        compiler_params=params(16),
        name="final_currents",
    )(incoming, expanded, parts, *fields)


def per_device(history, incident, proj_basis, expand_basis, near_inverse, couplings, lags):
    clusters, rank, unknowns = proj_basis.shape
    width = clusters * rank
    taps, src_rows, blocks = couplings.shape[:3]
    src_clusters = lags.shape[0]
    senders = src_rows // width
    flat = couplings.reshape(taps, src_rows * blocks, width)
    spread = jnp.repeat(jnp.eye(blocks * clusters, dtype=F32), rank, axis=1)
    lag_rows = jnp.dot(lags.reshape(src_clusters, blocks * clusters).astype(F32), spread)

    def gather(copies):
        return lax.all_to_all(copies, "src", 0, 0)

    def scatter(chunks):
        return lax.all_to_all(chunks, "obs", 0, 0)

    gathered = gather(project_history(history, proj_basis, senders))
    incoming, expanded, start, transfer = prepare_near(incident, expand_basis, near_inverse, proj_basis)
    w1, w2, w3, chunks, base = first_step(gathered, flat, lag_rows)
    fields, past = [], []
    ahead = None
    for step in range(STEPS):
        if step == 1:
            chunks = couple(step1_kernel, "step1", blocks, False, past[0], base, w1)
        elif step == 2:
            chunks, ahead = couple(step2_kernel, "step2", blocks, True, past[0], past[1], base, w1, w2)
        elif step == 3:
            chunks, ahead = couple(step3_kernel, "step3", blocks, True, *past, ahead, w1, w3)
        elif step == 4:
            chunks = couple(step4_kernel, "step4", blocks, False, past[2], past[3], ahead, w1, w2)
        parts = scatter(chunks)
        if step + 1 < STEPS:
            field, copies = project_step(parts, start, transfer, senders, step)
            fields.append(field)
            past.append(gather(copies))
    return final_currents(incoming, expanded, parts, fields)


def solution(mesh):
    placed = (
        P(None, ("obs", "src"), None, None),
        P(None, ("obs", "src"), None, None),
        P(("obs", "src"), None, None),
        P(("obs", "src"), None, None),
        P(("obs", "src"), None, None),
        P(None, "obs", None, "src", None),
        P("obs", None, "src", None),
    )
    return jax.shard_map(
        per_device,
        mesh=mesh,
        in_specs=placed,
        out_specs=P(None, ("obs", "src"), None, None),
        check_vma=False,
    )
```

```python
import functools

import jax
import jax.numpy as jnp
from jax import lax
from jax.experimental import pallas as pl
from jax.experimental.pallas import tpu as pltpu
from jax.sharding import PartitionSpec as P

STEPS = 5
HIST = 3
MIB = 1024 * 1024
BF16 = jnp.bfloat16
F32 = jnp.float32
ANY_SPEC = pl.BlockSpec(memory_space=pl.ANY)
VMEM_SPEC = pl.BlockSpec(memory_space=pltpu.VMEM)


def nt_dot(left, right):
    return lax.dot_general(left, right, (((1,), (1,)), ((), ())), preferred_element_type=F32)


def params(limit, **more):
    return pltpu.CompilerParams(vmem_limit_bytes=limit * MIB, **more)


def cost(flops, touched):
    return pl.CostEstimate(flops=int(flops), bytes_accessed=int(touched), transcendentals=0)


def history_kernel(history_ref, proj_ref, out_ref, held_ref, basis_ref, sems):
    slots, clusters, excite, unknowns = held_ref.shape
    copies = []
    for c in range(clusters):
        copies.append((
            pltpu.make_async_copy(proj_ref.at[c], basis_ref.at[c], sems.at[c, slots]),
            [pltpu.make_async_copy(history_ref.at[h, c], held_ref.at[h, c], sems.at[c, h]) for h in range(slots)],
        ))
    for basis, parts in copies:
        for part in parts:
            part.start()
        basis.start()
    sides = []
    for c, (basis, parts) in enumerate(copies):
        for part in parts:
            part.wait()
        basis.wait()
        left = jnp.concatenate([held_ref[h, c] for h in range(slots)], axis=0)
        sides.append(nt_dot(left, basis_ref[c]))
    both = jnp.concatenate(sides, axis=1).astype(BF16)
    for h in range(slots):
        out_ref[h] = both[h * excite:(h + 1) * excite]


def project_history(history, proj_basis):
    slots, clusters, excite, unknowns = history.shape
    rank = proj_basis.shape[1]
    return pl.pallas_call(
        history_kernel,
        out_shape=jax.ShapeDtypeStruct((slots, excite, clusters * rank), BF16),
        in_specs=[ANY_SPEC] * 2,
        out_specs=VMEM_SPEC,
        scratch_shapes=[
            pltpu.VMEM(history.shape, BF16),
            pltpu.VMEM(proj_basis.shape, BF16),
            pltpu.SemaphoreType.DMA((clusters, slots + 1)),
        ],
        compiler_params=params(8),
        name="project_history",
    )(in_hbm(history), in_hbm(proj_basis))


def order_kernel(stride, own_ref, by1_ref, by3_ref, by2_ref, out_ref):
    me = lax.rem(lax.axis_index("src") // stride, 4)
    for k, ref in ((0, own_ref), (1, by1_ref), (3, by3_ref), (2, by2_ref)):
        out_ref[me ^ k] = ref[...]


def exchange(array, stride, name):
    arrived = [
        lax.ppermute(array, "src", [(i, i ^ (k * stride)) for i in range(16)]) for k in (1, 3, 2)
    ]
    return pl.pallas_call(
        functools.partial(order_kernel, stride),
        out_shape=jax.ShapeDtypeStruct((4,) + array.shape, array.dtype),
        in_specs=[VMEM_SPEC] * 4,
        out_specs=VMEM_SPEC,
        compiler_params=params(8),
        name=name,
    )(array, *arrived)


def near_kernel(depth, incident_ref, expand_ref, near_ref, proj_ref,
                incoming_ref, expanded_ref, start_ref, transfer_ref,
                held_ref, tiles_ref, basis_ref, held_sems, tile_sems, basis_sems):
    steps, clusters, excite, unknowns = incident_ref.shape
    rank = expand_ref.shape[1]
    count, _, tile = tiles_ref.shape
    per = count // clusters
    head = steps * excite

    def held_copy(c):
        return [
            pltpu.make_async_copy(
                incident_ref.at[t, c], held_ref.at[c, pl.ds(t * excite, excite)], held_sems.at[c, t])
            for t in range(steps)
        ] + [pltpu.make_async_copy(expand_ref.at[c], held_ref.at[c, pl.ds(head, rank)], held_sems.at[c, steps])]

    def tile_copy(i):
        c, n = divmod(i, per)
        return pltpu.make_async_copy(near_ref.at[c, :, pl.ds(n * tile, tile)], tiles_ref.at[i], tile_sems.at[i])

    def basis_copy(c):
        return pltpu.make_async_copy(proj_ref.at[c], basis_ref.at[c], basis_sems.at[c])

    def fetch(i):
        if i < count:
            c, n = divmod(i, per)
            if n == 0:
                for copy in held_copy(c):
                    copy.start()
            tile_copy(i).start()
            if n == 0:
                basis_copy(c).start()

    for i in range(depth):
        fetch(i)
    small = []
    for c in range(clusters):
        for copy in held_copy(c):
            copy.wait()
        total = None
        for n in range(per):
            tile_copy(c * per + n).wait()
            fetch(c * per + n + depth)
            if n == 0:
                basis_copy(c).wait()
            lanes = slice(n * tile, (n + 1) * tile)
            product = jnp.dot(held_ref[c], tiles_ref[c * per + n], preferred_element_type=F32).astype(BF16)
            for t in range(steps):
                incoming_ref[t, c, :, lanes] = product[t * excite:(t + 1) * excite]
            expanded_ref[c, :, lanes] = product[head:]
            part = nt_dot(product, basis_ref[c, :, lanes])
            total = part if total is None else total + part
        small.append(total)
    for t in range(steps):
        rows = slice(t * excite, (t + 1) * excite)
        start_ref[t] = jnp.concatenate([part[rows] for part in small], axis=1)
    zero = jnp.zeros((rank, rank), F32)
    full = jnp.concatenate([
        jnp.concatenate([small[0][head:], zero], axis=1),
        jnp.concatenate([zero, small[1][head:]], axis=1),
    ], axis=0)
    high = full.astype(BF16)
    low = (full - high.astype(F32)).astype(BF16)
    transfer_ref[...] = jnp.concatenate([high, low], axis=0)


def prepare_near(incident, expand_basis, near_inverse, proj_basis, tile=512, depth=2):
    steps, clusters, excite, unknowns = incident.shape
    rank = proj_basis.shape[1]
    rows = steps * excite + rank
    tiles = clusters * unknowns // tile
    return pl.pallas_call(
        functools.partial(near_kernel, depth),
        out_shape=(
            jax.ShapeDtypeStruct((steps, clusters, excite, unknowns), BF16),
            jax.ShapeDtypeStruct((clusters, rank, unknowns), BF16),
            jax.ShapeDtypeStruct((steps, excite, clusters * rank), F32),
            jax.ShapeDtypeStruct((2 * clusters * rank, clusters * rank), BF16),
        ),
        in_specs=[ANY_SPEC] * 4,
        out_specs=[VMEM_SPEC] * 4,
        scratch_shapes=[
            pltpu.VMEM((clusters, rows, unknowns), BF16),
            pltpu.VMEM((tiles, unknowns, tile), BF16),
            pltpu.VMEM((clusters, rank, unknowns), BF16),
            pltpu.SemaphoreType.DMA((clusters, steps + 1)),
            pltpu.SemaphoreType.DMA((tiles,)),
            pltpu.SemaphoreType.DMA((clusters,)),
        ],
        compiler_params=params(24),
        cost_estimate=cost(2 * clusters * rows * unknowns * (unknowns + rank), 2 * clusters * unknowns * unknowns),
        name="prepare_near",
    )(*[in_hbm(x) for x in (incident, expand_basis, near_inverse, proj_basis)])


def build_kernel(depth, couplings_ref, lags_ref, w1_ref, w2_ref, w3_ref, held_ref, sems):
    taps, _, columns_here = couplings_ref.shape
    clusters, columns = lags_ref.shape
    rank = w1_ref.shape[0] // clusters
    blocks = columns // columns_here
    rows_in = 256
    group = rows_in // blocks
    pieces, part = held_ref.shape[0], held_ref.shape[2]
    clusters_here = clusters // pieces

    def piece_copy(i, p):
        return pltpu.make_async_copy(
            couplings_ref.at[p, pl.ds(i * part, part)], held_ref.at[i, p], sems.at[i, p])

    def fetch(i):
        if i < pieces:
            for p in range(taps):
                piece_copy(i, p).start()

    for i in range(depth):
        fetch(i)
    to = lax.broadcasted_iota(jnp.int32, (rows_in, rows_in), 0)
    source = lax.broadcasted_iota(jnp.int32, (rows_in, rows_in), 1)
    wanted = (to % group) * blocks + to // group
    perm = jnp.where(source == wanted, 1.0, 0.0).astype(BF16)

    for i in range(pieces):
        for p in range(taps):
            piece_copy(i, p).wait()
        fetch(i + depth)
        for j in range(clusters_here):
            cluster = i * clusters_here + j
            lag = lags_ref[cluster:cluster + 1, :]
            masks = []
            for delay in (1.0, 2.0):
                row = jnp.where(lag == delay, 1.0, 0.0)
                masks.append([
                    jnp.broadcast_to(row[:, o * 128:(o + 1) * 128], (group, 128)).astype(BF16)
                    for o in range(blocks)
                ])
            for g in range(rank // group):
                at = j * (rank * blocks) + g * rows_in
                pair = jnp.concatenate([held_ref[i, p, at:at + rows_in, :] for p in range(taps)], axis=1)
                ordered = jnp.dot(perm, pair, preferred_element_type=F32).astype(BF16)
                out = slice(cluster * rank + g * group, cluster * rank + (g + 1) * group)
                for o in range(blocks):
                    k0 = ordered[o * group:(o + 1) * group, :128]
                    k1 = ordered[o * group:(o + 1) * group, 128:]
                    m1, m2 = masks[0][o], masks[1][o]
                    lanes = slice(o * 128, (o + 1) * 128)
                    w1_ref[out, lanes] = k0 * m1
                    w2_ref[out, lanes] = k0 * m2 + k1 * m1
                    w3_ref[out, lanes] = k1 * m2


def build_matrices(couplings, lag_rows, pieces=4, depth=2):
    clusters, columns = lag_rows.shape
    taps, count, width = couplings.shape
    rows = count * width // columns
    return pl.pallas_call(
        functools.partial(build_kernel, depth),
        out_shape=[jax.ShapeDtypeStruct((rows, columns), BF16)] * 3,
        in_specs=[ANY_SPEC, VMEM_SPEC],
        out_specs=[VMEM_SPEC] * 3,
        scratch_shapes=[
            pltpu.VMEM((pieces, taps, count // pieces, width), BF16),
            pltpu.SemaphoreType.DMA((pieces, taps)),
        ],
        compiler_params=params(28),
        cost_estimate=cost(2 * taps * 256 * rows * columns, 10 * rows * columns),
        name="build_matrices",
    )(in_hbm(couplings), lag_rows)


def in_hbm(array):
    return pltpu.with_memory_space_constraint(array, pltpu.HBM)


def wide(gathered_ref):
    return jnp.concatenate([gathered_ref[s] for s in range(gathered_ref.shape[0])], axis=1)


def send_field(field_ref, total):
    for o in range(field_ref.shape[0]):
        field_ref[o] = total[:, o * 128:(o + 1) * 128].astype(BF16)


def step0_kernel(history_ref, transfer_ref, w1_ref, w2_ref, w3_ref, field_ref, base_ref):
    excite = base_ref.shape[1]
    old, middle, new = [
        jnp.concatenate([history_ref[y, x, h] for y in range(4) for x in range(4)], axis=1)
        for h in range(HIST)
    ]
    one = jnp.dot(new, w1_ref[...], preferred_element_type=F32)
    two = jnp.dot(jnp.concatenate([middle, new], axis=0), w2_ref[...], preferred_element_type=F32)
    three = jnp.dot(jnp.concatenate([old, middle, new], axis=0), w3_ref[...], preferred_element_type=F32)
    send_field(field_ref, one + two[:excite] + three[:excite])
    base_ref[0] = two[excite:] + three[excite:2 * excite]
    base_ref[1] = three[2 * excite:]


def step1_kernel(q0_ref, base_ref, w1_ref, field_ref):
    send_field(field_ref, base_ref[0] + jnp.dot(wide(q0_ref), w1_ref[...], preferred_element_type=F32))


def step2_kernel(q0_ref, q1_ref, base_ref, w1_ref, w2_ref, field_ref, next_ref):
    excite = base_ref.shape[1]
    one, zero = wide(q1_ref), wide(q0_ref)
    two = jnp.dot(jnp.concatenate([zero, one], axis=0), w2_ref[...], preferred_element_type=F32)
    send_field(field_ref, base_ref[1] + two[:excite] + jnp.dot(one, w1_ref[...], preferred_element_type=F32))
    next_ref[...] = two[excite:]


def step3_kernel(q0_ref, q1_ref, q2_ref, base_ref, w1_ref, w3_ref, field_ref, next_ref):
    excite = base_ref.shape[0]
    three = jnp.dot(jnp.concatenate([wide(q0_ref), wide(q1_ref)], axis=0), w3_ref[...], preferred_element_type=F32)
    send_field(field_ref, base_ref[...] + three[:excite]
               + jnp.dot(wide(q2_ref), w1_ref[...], preferred_element_type=F32))
    next_ref[...] = three[excite:]


def step4_kernel(q2_ref, q3_ref, base_ref, w1_ref, w2_ref, field_ref):
    send_field(field_ref, base_ref[...]
               + jnp.dot(wide(q2_ref), w2_ref[...], preferred_element_type=F32)
               + jnp.dot(wide(q3_ref), w1_ref[...], preferred_element_type=F32))


def couple(kernel, name, blocks, extra, gathered, bases, weights):
    excite, width = gathered[0].shape[-2:]
    shapes = [jax.ShapeDtypeStruct((blocks, excite, width), BF16)]
    if extra:
        shapes.append(jax.ShapeDtypeStruct(extra, F32))
    got = pl.pallas_call(
        kernel,
        out_shape=shapes,
        in_specs=[VMEM_SPEC] * (len(gathered) + len(bases) + len(weights)),
        out_specs=[VMEM_SPEC] * len(shapes),
        compiler_params=params(16),
        name=name,
    )(*gathered, *bases, *weights)
    return got if extra else got[0]


def project_kernel(parts_ref, start_ref, transfer_ref, field_ref, out_ref):
    total = parts_ref[0].astype(F32)
    for o in range(1, parts_ref.shape[0]):
        total = total + parts_ref[o].astype(F32)
    field = total.astype(BF16)
    field_ref[...] = field
    q = start_ref[0] - jnp.dot(
        jnp.concatenate([field, field], axis=1), transfer_ref[...], preferred_element_type=F32)
    q = q.astype(BF16)
    for s in range(out_ref.shape[0]):
        out_ref[s] = q


def project_step(parts, start, transfer, copies, step):
    blocks, excite, width = parts.shape
    return pl.pallas_call(
        project_kernel,
        grid=(1,),
        out_shape=(
            jax.ShapeDtypeStruct((excite, width), BF16),
            jax.ShapeDtypeStruct((copies, excite, width), BF16),
        ),
        in_specs=[
            pl.BlockSpec(parts.shape, lambda i: (0, 0, 0)),
            pl.BlockSpec((1, excite, width), lambda i: (step, 0, 0)),
            pl.BlockSpec(transfer.shape, lambda i: (0, 0)),
        ],
        out_specs=(
            pl.BlockSpec((excite, width), lambda i: (0, 0)),
            pl.BlockSpec((copies, excite, width), lambda i: (0, 0, 0)),
        ),
        compiler_params=params(8),
        name="project_step",
    )(parts, start, transfer)


def currents_kernel(incoming_ref, expanded_ref, parts_ref, f0_ref, f1_ref, f2_ref, f3_ref, out_ref):
    total = parts_ref[0].astype(F32)
    for o in range(1, parts_ref.shape[0]):
        total = total + parts_ref[o].astype(F32)
    fields = [f0_ref[...], f1_ref[...], f2_ref[...], f3_ref[...], total.astype(BF16)]
    excite = out_ref.shape[2]
    rank = expanded_ref.shape[1]
    for c in range(out_ref.shape[1]):
        left = jnp.concatenate([f[:, c * rank:(c + 1) * rank] for f in fields], axis=0)
        far = jnp.dot(left, expanded_ref[c], preferred_element_type=F32)
        for t in range(out_ref.shape[0]):
            out_ref[t, c] = (incoming_ref[t, c].astype(F32) - far[t * excite:(t + 1) * excite]).astype(BF16)


def final_currents(incoming, expanded, parts, fields, tile=512):
    steps, clusters, excite, unknowns = incoming.shape
    rank = expanded.shape[1]
    small = pl.BlockSpec(fields[0].shape, lambda n: (0, 0))
    return pl.pallas_call(
        currents_kernel,
        grid=(unknowns // tile,),
        out_shape=jax.ShapeDtypeStruct(incoming.shape, BF16),
        in_specs=[
            pl.BlockSpec((steps, clusters, excite, tile), lambda n: (0, 0, 0, n)),
            pl.BlockSpec((clusters, rank, tile), lambda n: (0, 0, n)),
            pl.BlockSpec(parts.shape, lambda n: (0, 0, 0)),
        ] + [small] * len(fields),
        out_specs=pl.BlockSpec((steps, clusters, excite, tile), lambda n: (0, 0, 0, n)),
        compiler_params=params(16),
        name="final_currents",
    )(incoming, expanded, parts, *fields)


def per_device(history, incident, proj_basis, expand_basis, near_inverse, couplings, lags):
    clusters, rank, unknowns = proj_basis.shape
    width = clusters * rank
    taps, src_rows, blocks = couplings.shape[:3]
    src_clusters = lags.shape[0]
    senders = src_rows // width
    flat = couplings.reshape(taps, src_rows * blocks, width)
    spread = jnp.repeat(jnp.eye(blocks * clusters, dtype=F32), rank, axis=1)
    lag_rows = jnp.dot(lags.reshape(src_clusters, blocks * clusters).astype(F32), spread)

    def gather(copies):
        return lax.all_to_all(copies, "src", 0, 0)

    def scatter(chunks):
        return lax.all_to_all(chunks, "obs", 0, 0)

    mine = project_history(history, proj_basis)
    gathered = exchange(exchange(mine, 1, "order_x"), 4, "order_y")
    incoming, expanded, start, transfer = prepare_near(incident, expand_basis, near_inverse, proj_basis)
    w1, w2, w3 = build_matrices(flat, lag_rows)
    fields, past = [], []
    excite = history.shape[2]
    full = (excite, blocks * width)
    ahead = None
    for step in range(STEPS):
        if step == 0:
            chunks, base = couple(step0_kernel, "step0", blocks, (2,) + full, [gathered], [transfer], [w1, w2, w3])
        elif step == 1:
            chunks = couple(step1_kernel, "step1", blocks, None, past, [base], [w1])
        elif step == 2:
            chunks, ahead = couple(step2_kernel, "step2", blocks, full, past, [base], [w1, w2])
        elif step == 3:
            chunks, ahead = couple(step3_kernel, "step3", blocks, full, past, [ahead], [w1, w3])
        else:
            chunks = couple(step4_kernel, "step4", blocks, None, past[2:], [ahead], [w1, w2])
        parts = scatter(chunks)
        if step + 1 < STEPS:
            field, copies = project_step(parts, start, transfer, senders, step)
            fields.append(field)
            past.append(gather(copies))
    return final_currents(incoming, expanded, parts, fields)


def solution(mesh):
    placed = (
        P(None, ("obs", "src"), None, None),
        P(None, ("obs", "src"), None, None),
        P(("obs", "src"), None, None),
        P(("obs", "src"), None, None),
        P(("obs", "src"), None, None),
        P(None, "obs", None, "src", None),
        P("obs", None, "src", None),
    )
    return jax.shard_map(
        per_device,
        mesh=mesh,
        in_specs=placed,
        out_specs=P(None, ("obs", "src"), None, None),
        check_vma=False,
    )
```

```python
import functools

import jax
import jax.numpy as jnp
from jax import lax
from jax.experimental import pallas as pl
from jax.experimental.pallas import tpu as pltpu
from jax.sharding import PartitionSpec as P

STEPS = 5
HIST = 3
TOP = 5
MIB = 1024 * 1024
BF16 = jnp.bfloat16
F32 = jnp.float32
ANY_SPEC = pl.BlockSpec(memory_space=pl.ANY)
VMEM_SPEC = pl.BlockSpec(memory_space=pltpu.VMEM)


def nt_dot(left, right):
    return lax.dot_general(left, right, (((1,), (1,)), ((), ())), preferred_element_type=F32)


def params(limit, **more):
    return pltpu.CompilerParams(vmem_limit_bytes=limit * MIB, **more)


def cost(flops, touched):
    return pl.CostEstimate(flops=int(flops), bytes_accessed=int(touched), transcendentals=0)


def history_kernel(history_ref, proj_ref, lags_ref, out_ref, spread_ref, held_ref, basis_ref, pairs_ref, sems, pairs_sem):
    slots, clusters, excite, unknowns = held_ref.shape
    blocks, observers, sources = lags_ref.shape
    columns = spread_ref.shape[1]
    pairs_copy = pltpu.make_async_copy(lags_ref, pairs_ref, pairs_sem)
    pairs_copy.start()
    copies = []
    for c in range(clusters):
        copies.append((
            pltpu.make_async_copy(proj_ref.at[c], basis_ref.at[c], sems.at[c, slots]),
            [pltpu.make_async_copy(history_ref.at[h, c], held_ref.at[h, c], sems.at[c, h]) for h in range(slots)],
        ))
    for basis, parts in copies:
        for part in parts:
            part.start()
        basis.start()
    pairs_copy.wait()
    pairs = jnp.concatenate([pairs_ref[o] for o in range(blocks)], axis=0).astype(F32)
    owner = lax.broadcasted_iota(jnp.int32, (blocks * observers, columns), 1) // (columns // (blocks * observers))
    row = lax.broadcasted_iota(jnp.int32, (blocks * observers, columns), 0)
    spread_ref[...] = lax.dot_general(
        pairs, jnp.where(owner == row, 1.0, 0.0), (((0,), (0,)), ((), ())), preferred_element_type=F32)
    sides = []
    for c, (basis, parts) in enumerate(copies):
        for part in parts:
            part.wait()
        basis.wait()
        left = jnp.concatenate([held_ref[h, c] for h in range(slots)], axis=0)
        sides.append(nt_dot(left, basis_ref[c]))
    both = jnp.concatenate(sides, axis=1).astype(BF16)
    for h in range(slots):
        out_ref[h] = both[h * excite:(h + 1) * excite]


def project_history(history, proj_basis, lags):
    slots, clusters, excite, unknowns = history.shape
    rank = proj_basis.shape[1]
    blocks, observers, sources = lags.shape
    return pl.pallas_call(
        history_kernel,
        out_shape=(
            jax.ShapeDtypeStruct((slots, excite, clusters * rank), BF16),
            jax.ShapeDtypeStruct((sources, blocks * observers * rank), F32),
        ),
        in_specs=[ANY_SPEC] * 3,
        out_specs=[VMEM_SPEC] * 2,
        scratch_shapes=[
            pltpu.VMEM(history.shape, BF16),
            pltpu.VMEM(proj_basis.shape, BF16),
            pltpu.VMEM(lags.shape, lags.dtype),
            pltpu.SemaphoreType.DMA((clusters, slots + 1)),
            pltpu.SemaphoreType.DMA,
        ],
        compiler_params=params(8),
        name="project_history",
    )(in_hbm(history), in_hbm(proj_basis), in_hbm(lags))


def order_kernel(stride, own_ref, by1_ref, by3_ref, by2_ref, after_ref, out_ref):
    me = lax.rem(lax.axis_index("src") // stride, 4)
    for k, ref in ((0, own_ref), (1, by1_ref), (3, by3_ref), (2, by2_ref)):
        out_ref[me ^ k] = ref[...]


def swap(array, stride):
    return [lax.ppermute(array, "src", [(i, i ^ (k * stride)) for i in range(16)]) for k in (1, 3, 2)]


def ordered(array, arrived, after, stride, name):
    return pl.pallas_call(
        functools.partial(order_kernel, stride),
        out_shape=jax.ShapeDtypeStruct((4,) + array.shape, array.dtype),
        in_specs=[VMEM_SPEC] * 4 + [ANY_SPEC],
        out_specs=VMEM_SPEC,
        compiler_params=params(8),
        name=name,
    )(array, *arrived, after)


def near_kernel(tile, incident_ref, expand_ref, near_ref, proj_ref, after_ref,
                incoming_ref, expanded_ref, start_ref, transfer_ref):
    steps, clusters, excite, unknowns = incident_ref.shape
    rank = expand_ref.shape[1]
    head = steps * excite
    small = []
    for c in range(clusters):
        left = jnp.concatenate([incident_ref[t, c] for t in range(steps)] + [expand_ref[c]], axis=0)
        total = None
        for n in range(unknowns // tile):
            lanes = slice(n * tile, (n + 1) * tile)
            product = jnp.dot(left, near_ref[c, :, lanes], preferred_element_type=F32).astype(BF16)
            for t in range(steps):
                incoming_ref[t, c, :, lanes] = product[t * excite:(t + 1) * excite]
            expanded_ref[c, :, lanes] = product[head:]
            part = nt_dot(product, proj_ref[c, :, lanes])
            total = part if total is None else total + part
        small.append(total)
    for t in range(steps):
        rows = slice(t * excite, (t + 1) * excite)
        start_ref[t] = jnp.concatenate([part[rows] for part in small], axis=1)
    zero = jnp.zeros((rank, rank), F32)
    full = jnp.concatenate([
        jnp.concatenate([small[0][head:], zero], axis=1),
        jnp.concatenate([zero, small[1][head:]], axis=1),
    ], axis=0)
    high = full.astype(BF16)
    low = (full - high.astype(F32)).astype(BF16)
    transfer_ref[...] = jnp.concatenate([high, low], axis=0)


def prepare_near(incident, expand_basis, near_inverse, proj_basis, after, tile=512):
    steps, clusters, excite, unknowns = incident.shape
    rank = proj_basis.shape[1]
    rows = steps * excite + rank
    return pl.pallas_call(
        functools.partial(near_kernel, tile),
        out_shape=(
            jax.ShapeDtypeStruct((steps, clusters, excite, unknowns), BF16),
            jax.ShapeDtypeStruct((clusters, rank, unknowns), BF16),
            jax.ShapeDtypeStruct((steps, excite, clusters * rank), F32),
            jax.ShapeDtypeStruct((2 * clusters * rank, clusters * rank), BF16),
        ),
        in_specs=[VMEM_SPEC] * 4 + [ANY_SPEC],
        out_specs=[VMEM_SPEC] * 4,
        compiler_params=params(20),
        cost_estimate=cost(2 * clusters * rows * unknowns * (unknowns + rank), 2 * clusters * unknowns * unknowns),
        name="prepare_near",
    )(incident, expand_basis, near_inverse, proj_basis, after)


def build_kernel(first, rank, depth, couplings_ref, spread_ref, after_ref, w1_ref, w2_ref, w3_ref, held_ref, sems):
    taps, _, columns_here = couplings_ref.shape
    columns = w1_ref.shape[1]
    blocks = columns // columns_here
    rows_in = 256
    group = rows_in // blocks
    pieces, part = held_ref.shape[0], held_ref.shape[2]
    clusters_here = part // (rank * blocks)

    def piece_copy(i, p):
        return pltpu.make_async_copy(
            couplings_ref.at[p, pl.ds(first * rank * blocks + i * part, part)], held_ref.at[i, p], sems.at[i, p])

    def fetch(i):
        if i < pieces:
            for p in range(taps):
                piece_copy(i, p).start()

    for i in range(depth):
        fetch(i)
    to = lax.broadcasted_iota(jnp.int32, (rows_in, rows_in), 0)
    source = lax.broadcasted_iota(jnp.int32, (rows_in, rows_in), 1)
    wanted = (to % group) * blocks + to // group
    perm = jnp.where(source == wanted, 1.0, 0.0).astype(BF16)

    for i in range(pieces):
        for p in range(taps):
            piece_copy(i, p).wait()
        fetch(i + depth)
        for j in range(clusters_here):
            cluster = i * clusters_here + j
            lag = spread_ref[first + cluster:first + cluster + 1, :]
            masks = []
            for delay in (1.0, 2.0):
                row = jnp.where(lag == delay, 1.0, 0.0)
                masks.append([
                    jnp.broadcast_to(row[:, o * 128:(o + 1) * 128], (group, 128)).astype(BF16)
                    for o in range(blocks)
                ])
            for g in range(rank // group):
                at = j * (rank * blocks) + g * rows_in
                pair = jnp.concatenate([held_ref[i, p, at:at + rows_in, :] for p in range(taps)], axis=1)
                ordered = jnp.dot(perm, pair, preferred_element_type=F32).astype(BF16)
                out = slice(cluster * rank + g * group, cluster * rank + (g + 1) * group)
                for o in range(blocks):
                    k0 = ordered[o * group:(o + 1) * group, :128]
                    k1 = ordered[o * group:(o + 1) * group, 128:]
                    m1, m2 = masks[0][o], masks[1][o]
                    lanes = slice(o * 128, (o + 1) * 128)
                    w1_ref[out, lanes] = k0 * m1
                    w2_ref[out, lanes] = k0 * m2 + k1 * m1
                    w3_ref[out, lanes] = k1 * m2


def build_matrices(first, pieces, couplings, spread, after, depth=3, clusters_here=4):
    sources, columns = spread.shape
    taps, count, width = couplings.shape
    blocks = columns // width
    rank = count // blocks // sources
    matrix = jax.ShapeDtypeStruct((pieces * clusters_here * rank, columns), BF16)
    return pl.pallas_call(
        functools.partial(build_kernel, first, rank, depth),
        out_shape=[matrix] * 3,
        in_specs=[ANY_SPEC, VMEM_SPEC, ANY_SPEC],
        out_specs=[VMEM_SPEC] * 3,
        scratch_shapes=[
            pltpu.VMEM((pieces, taps, clusters_here * rank * blocks, width), BF16),
            pltpu.SemaphoreType.DMA((pieces, taps)),
        ],
        compiler_params=params(20),
        cost_estimate=cost(6 * taps * 256 * matrix.size, 10 * matrix.size),
        name=f"build_matrices{first}",
    )(in_hbm(couplings), spread, after)


def in_hbm(array):
    return pltpu.with_memory_space_constraint(array, pltpu.HBM)


def wide(gathered_ref):
    return jnp.concatenate([gathered_ref[s] for s in range(gathered_ref.shape[0])], axis=1)


def send_field(field_ref, total):
    for o in range(field_ref.shape[0]):
        field_ref[o] = total[:, o * 128:(o + 1) * 128].astype(BF16)


def apply(left, top_ref, bottom_ref):
    half = top_ref.shape[0]
    return (jnp.dot(left[:, :half], top_ref[...], preferred_element_type=F32)
            + jnp.dot(left[:, half:], bottom_ref[...], preferred_element_type=F32))


def step0_kernel(history_ref, transfer_ref, w1a_ref, w1b_ref, w2a_ref, w2b_ref, w3a_ref, w3b_ref,
                 field_ref, base_ref):
    excite = base_ref.shape[1]
    old, middle, new = [
        jnp.concatenate([history_ref[y, x, h] for y in range(4) for x in range(4)], axis=1)
        for h in range(HIST)
    ]
    one = apply(new, w1a_ref, w1b_ref)
    two = apply(jnp.concatenate([middle, new], axis=0), w2a_ref, w2b_ref)
    three = apply(jnp.concatenate([old, middle, new], axis=0), w3a_ref, w3b_ref)
    send_field(field_ref, one + two[:excite] + three[:excite])
    base_ref[0] = two[excite:] + three[excite:2 * excite]
    base_ref[1] = three[2 * excite:]


def step1_kernel(q0_ref, base_ref, w1a_ref, w1b_ref, field_ref):
    send_field(field_ref, base_ref[0] + apply(wide(q0_ref), w1a_ref, w1b_ref))


def step2_kernel(q0_ref, q1_ref, base_ref, w1a_ref, w1b_ref, w2a_ref, w2b_ref, field_ref, next_ref):
    excite = base_ref.shape[1]
    one, zero = wide(q1_ref), wide(q0_ref)
    two = apply(jnp.concatenate([zero, one], axis=0), w2a_ref, w2b_ref)
    send_field(field_ref, base_ref[1] + two[:excite] + apply(one, w1a_ref, w1b_ref))
    next_ref[...] = two[excite:]


def step3_kernel(q0_ref, q1_ref, q2_ref, base_ref, w1a_ref, w1b_ref, w3a_ref, w3b_ref, field_ref, next_ref):
    excite = base_ref.shape[0]
    three = apply(jnp.concatenate([wide(q0_ref), wide(q1_ref)], axis=0), w3a_ref, w3b_ref)
    send_field(field_ref, base_ref[...] + three[:excite] + apply(wide(q2_ref), w1a_ref, w1b_ref))
    next_ref[...] = three[excite:]


def step4_kernel(q2_ref, q3_ref, base_ref, w1a_ref, w1b_ref, w2a_ref, w2b_ref, field_ref):
    send_field(field_ref, base_ref[...] + apply(wide(q2_ref), w2a_ref, w2b_ref)
               + apply(wide(q3_ref), w1a_ref, w1b_ref))


def couple(kernel, name, blocks, extra, gathered, bases, weights):
    excite, width = gathered[0].shape[-2:]
    shapes = [jax.ShapeDtypeStruct((blocks, excite, width), BF16)]
    if extra:
        shapes.append(jax.ShapeDtypeStruct(extra, F32))
    got = pl.pallas_call(
        kernel,
        out_shape=shapes,
        in_specs=[VMEM_SPEC] * (len(gathered) + len(bases) + len(weights)),
        out_specs=[VMEM_SPEC] * len(shapes),
        compiler_params=params(16),
        name=name,
    )(*gathered, *bases, *weights)
    return got if extra else got[0]


def project_kernel(parts_ref, start_ref, transfer_ref, field_ref, out_ref):
    total = parts_ref[0].astype(F32)
    for o in range(1, parts_ref.shape[0]):
        total = total + parts_ref[o].astype(F32)
    field = total.astype(BF16)
    field_ref[...] = field
    q = start_ref[0] - jnp.dot(
        jnp.concatenate([field, field], axis=1), transfer_ref[...], preferred_element_type=F32)
    q = q.astype(BF16)
    for s in range(out_ref.shape[0]):
        out_ref[s] = q


def project_step(parts, start, transfer, copies, step):
    blocks, excite, width = parts.shape
    return pl.pallas_call(
        project_kernel,
        grid=(1,),
        out_shape=(
            jax.ShapeDtypeStruct((excite, width), BF16),
            jax.ShapeDtypeStruct((copies, excite, width), BF16),
        ),
        in_specs=[
            pl.BlockSpec(parts.shape, lambda i: (0, 0, 0)),
            pl.BlockSpec((1, excite, width), lambda i: (step, 0, 0)),
            pl.BlockSpec(transfer.shape, lambda i: (0, 0)),
        ],
        out_specs=(
            pl.BlockSpec((excite, width), lambda i: (0, 0)),
            pl.BlockSpec((copies, excite, width), lambda i: (0, 0, 0)),
        ),
        compiler_params=params(8),
        name="project_step",
    )(parts, start, transfer)


def summed(parts_ref):
    total = parts_ref[0].astype(F32)
    for o in range(1, parts_ref.shape[0]):
        total = total + parts_ref[o].astype(F32)
    return total.astype(BF16)


def currents_kernel(incoming_ref, expanded_ref, parts_ref,
                    f0_ref, f1_ref, f2_ref, f3_ref, out_ref, made_ref, sems):
    fields = [f0_ref[...], f1_ref[...], f2_ref[...], f3_ref[...], summed(parts_ref)]
    clusters, pieces, steps, excite, tile = made_ref.shape
    rank = expanded_ref.shape[1]
    copies = []
    for c in range(clusters):
        left = jnp.concatenate([f[:, c * rank:(c + 1) * rank] for f in fields], axis=0)
        for n in range(pieces):
            lanes = slice(n * tile, (n + 1) * tile)
            far = jnp.dot(left, expanded_ref[c, :, lanes], preferred_element_type=F32)
            for t in range(steps):
                made_ref[c, n, t] = (
                    incoming_ref[t, c, :, lanes].astype(F32) - far[t * excite:(t + 1) * excite]).astype(BF16)
            copy = pltpu.make_async_copy(
                made_ref.at[c, n], out_ref.at[:, c, :, pl.ds(n * tile, tile)], sems.at[c, n])
            copy.start()
            copies.append(copy)
    for copy in copies:
        copy.wait()


def final_currents(incoming, expanded, parts, fields, tile=512):
    steps, clusters, excite, unknowns = incoming.shape
    return pl.pallas_call(
        currents_kernel,
        out_shape=jax.ShapeDtypeStruct((steps, clusters, excite, unknowns), BF16),
        in_specs=[VMEM_SPEC] * (3 + len(fields)),
        out_specs=ANY_SPEC,
        scratch_shapes=[
            pltpu.VMEM((clusters, unknowns // tile, steps, excite, tile), BF16),
            pltpu.SemaphoreType.DMA((clusters, unknowns // tile)),
        ],
        compiler_params=params(12),
        name="final_currents",
    )(incoming, expanded, parts, *fields)


def per_device(history, incident, proj_basis, expand_basis, near_inverse, couplings, lags):
    clusters, rank, unknowns = proj_basis.shape
    width = clusters * rank
    taps, src_rows, blocks = couplings.shape[:3]
    pairs = lags.transpose(1, 2, 3, 0)[:, 0]
    senders = src_rows // width
    flat = couplings.reshape(taps, src_rows * blocks, width)
    def gather(copies):
        return lax.all_to_all(copies, "src", 0, 0)

    def scatter(chunks):
        return lax.all_to_all(chunks, "obs", 0, 0)

    mine, spread = project_history(history, proj_basis, pairs)
    arrived = swap(mine, 1)
    top = build_matrices(0, TOP, flat, spread, mine)
    mine = ordered(mine, arrived, top[0], 1, "order_x")
    arrived = swap(mine, 4)
    bottom = build_matrices(4 * TOP, 8 - TOP, flat, spread, mine)
    incoming, expanded, start, transfer = prepare_near(incident, expand_basis, near_inverse, proj_basis, bottom[0])
    w1, w2, w3 = [list(halves) for halves in zip(top, bottom)]
    gathered = ordered(mine, arrived, transfer, 4, "order_y")
    fields, past = [], []
    excite = history.shape[2]
    full = (excite, blocks * width)
    ahead = None
    for step in range(STEPS):
        if step == 0:
            chunks, base = couple(step0_kernel, "step0", blocks, (2,) + full, [gathered], [transfer], w1 + w2 + w3)
        elif step == 1:
            chunks = couple(step1_kernel, "step1", blocks, None, past, [base], w1)
        elif step == 2:
            chunks, ahead = couple(step2_kernel, "step2", blocks, full, past, [base], w1 + w2)
        elif step == 3:
            chunks, ahead = couple(step3_kernel, "step3", blocks, full, past, [ahead], w1 + w3)
        else:
            chunks = couple(step4_kernel, "step4", blocks, None, past[2:], [ahead], w1 + w2)
        parts = scatter(chunks)
        if step + 1 < STEPS:
            field, copies = project_step(parts, start, transfer, senders, step)
            fields.append(field)
            past.append(gather(copies))
    return final_currents(incoming, expanded, parts, fields)


def solution(mesh):
    placed = (
        P(None, ("obs", "src"), None, None),
        P(None, ("obs", "src"), None, None),
        P(("obs", "src"), None, None),
        P(("obs", "src"), None, None),
        P(("obs", "src"), None, None),
        P(None, "obs", None, "src", None),
        P("obs", None, "src", None),
    )
    return jax.shard_map(
        per_device,
        mesh=mesh,
        in_specs=placed,
        out_specs=P(None, ("obs", "src"), None, None),
        check_vma=False,
    )
```

```python
import functools

import jax
import jax.numpy as jnp
from jax import lax
from jax.experimental import pallas as pl
from jax.experimental.pallas import tpu as pltpu
from jax.sharding import PartitionSpec as P

STEPS = 5
HIST = 3
TOP = 5
MIB = 1024 * 1024
BF16 = jnp.bfloat16
F32 = jnp.float32
ANY_SPEC = pl.BlockSpec(memory_space=pl.ANY)
VMEM_SPEC = pl.BlockSpec(memory_space=pltpu.VMEM)


def nt_dot(left, right):
    return lax.dot_general(left, right, (((1,), (1,)), ((), ())), preferred_element_type=F32)


def params(limit, **more):
    return pltpu.CompilerParams(vmem_limit_bytes=limit * MIB, **more)


def cost(flops, touched):
    return pl.CostEstimate(flops=int(flops), bytes_accessed=int(touched), transcendentals=0)


def history_kernel(history_ref, proj_ref, lags_ref, out_ref, spread_ref, held_ref, basis_ref, pairs_ref, sems, pairs_sem):
    slots, clusters, excite, unknowns = held_ref.shape
    blocks, observers, sources = lags_ref.shape
    columns = spread_ref.shape[1]
    pairs_copy = pltpu.make_async_copy(lags_ref, pairs_ref, pairs_sem)
    pairs_copy.start()
    copies = []
    for c in range(clusters):
        copies.append((
            pltpu.make_async_copy(proj_ref.at[c], basis_ref.at[c], sems.at[c, slots]),
            [pltpu.make_async_copy(history_ref.at[h, c], held_ref.at[h, c], sems.at[c, h]) for h in range(slots)],
        ))
    for basis, parts in copies:
        for part in parts:
            part.start()
        basis.start()
    pairs_copy.wait()
    pairs = jnp.concatenate([pairs_ref[o] for o in range(blocks)], axis=0).astype(F32)
    owner = lax.broadcasted_iota(jnp.int32, (blocks * observers, columns), 1) // (columns // (blocks * observers))
    row = lax.broadcasted_iota(jnp.int32, (blocks * observers, columns), 0)
    spread_ref[...] = lax.dot_general(
        pairs, jnp.where(owner == row, 1.0, 0.0), (((0,), (0,)), ((), ())), preferred_element_type=F32)
    sides = []
    for c, (basis, parts) in enumerate(copies):
        for part in parts:
            part.wait()
        basis.wait()
        left = jnp.concatenate([held_ref[h, c] for h in range(slots)], axis=0)
        sides.append(nt_dot(left, basis_ref[c]))
    both = jnp.concatenate(sides, axis=1).astype(BF16)
    for h in range(slots):
        out_ref[h] = both[h * excite:(h + 1) * excite]


def project_history(history, proj_basis, lags):
    slots, clusters, excite, unknowns = history.shape
    rank = proj_basis.shape[1]
    blocks, observers, sources = lags.shape
    return pl.pallas_call(
        history_kernel,
        out_shape=(
            jax.ShapeDtypeStruct((slots, excite, clusters * rank), BF16),
            jax.ShapeDtypeStruct((sources, blocks * observers * rank), F32),
        ),
        in_specs=[ANY_SPEC] * 3,
        out_specs=[VMEM_SPEC] * 2,
        scratch_shapes=[
            pltpu.VMEM(history.shape, BF16),
            pltpu.VMEM(proj_basis.shape, BF16),
            pltpu.VMEM(lags.shape, lags.dtype),
            pltpu.SemaphoreType.DMA((clusters, slots + 1)),
            pltpu.SemaphoreType.DMA,
        ],
        compiler_params=params(8),
        name="project_history",
    )(in_hbm(history), in_hbm(proj_basis), in_hbm(lags))


def order_kernel(stride, own_ref, by1_ref, by3_ref, by2_ref, after_ref, out_ref):
    me = lax.rem(lax.axis_index("src") // stride, 4)
    for k, ref in ((0, own_ref), (1, by1_ref), (3, by3_ref), (2, by2_ref)):
        out_ref[me ^ k] = ref[...]


def swap(array, stride):
    return [lax.ppermute(array, "src", [(i, i ^ (k * stride)) for i in range(16)]) for k in (1, 3, 2)]


def ordered(array, arrived, after, stride, name):
    return pl.pallas_call(
        functools.partial(order_kernel, stride),
        out_shape=jax.ShapeDtypeStruct((4,) + array.shape, array.dtype),
        in_specs=[VMEM_SPEC] * 4 + [ANY_SPEC],
        out_specs=VMEM_SPEC,
        compiler_params=params(8),
        name=name,
    )(array, *arrived, after)


def near_kernel(tile, incident_ref, expand_ref, near_ref, proj_ref, after_ref,
                incoming_ref, expanded_ref, start_ref, transfer_ref):
    steps, clusters, excite, unknowns = incident_ref.shape
    rank = expand_ref.shape[1]
    head = steps * excite
    small = []
    for c in range(clusters):
        left = jnp.concatenate([incident_ref[t, c] for t in range(steps)] + [expand_ref[c]], axis=0)
        total = None
        for n in range(unknowns // tile):
            lanes = slice(n * tile, (n + 1) * tile)
            product = jnp.dot(left, near_ref[c, :, lanes], preferred_element_type=F32).astype(BF16)
            for t in range(steps):
                incoming_ref[t, c, :, lanes] = product[t * excite:(t + 1) * excite]
            expanded_ref[c, :, lanes] = product[head:]
            part = nt_dot(product, proj_ref[c, :, lanes])
            total = part if total is None else total + part
        small.append(total)
    for t in range(steps):
        rows = slice(t * excite, (t + 1) * excite)
        start_ref[t] = jnp.concatenate([part[rows] for part in small], axis=1)
    zero = jnp.zeros((rank, rank), F32)
    full = jnp.concatenate([
        jnp.concatenate([small[0][head:], zero], axis=1),
        jnp.concatenate([zero, small[1][head:]], axis=1),
    ], axis=0)
    high = full.astype(BF16)
    low = (full - high.astype(F32)).astype(BF16)
    transfer_ref[...] = jnp.concatenate([high, low], axis=0)


def prepare_near(incident, expand_basis, near_inverse, proj_basis, after, tile=512):
    steps, clusters, excite, unknowns = incident.shape
    rank = proj_basis.shape[1]
    rows = steps * excite + rank
    return pl.pallas_call(
        functools.partial(near_kernel, tile),
        out_shape=(
            jax.ShapeDtypeStruct((steps, clusters, excite, unknowns), BF16),
            jax.ShapeDtypeStruct((clusters, rank, unknowns), BF16),
            jax.ShapeDtypeStruct((steps, excite, clusters * rank), F32),
            jax.ShapeDtypeStruct((2 * clusters * rank, clusters * rank), BF16),
        ),
        in_specs=[VMEM_SPEC] * 4 + [ANY_SPEC],
        out_specs=[VMEM_SPEC] * 4,
        compiler_params=params(20),
        cost_estimate=cost(2 * clusters * rows * unknowns * (unknowns + rank), 2 * clusters * unknowns * unknowns),
        name="prepare_near",
    )(incident, expand_basis, near_inverse, proj_basis, after)


def build_kernel(first, rank, depth, couplings_ref, spread_ref, after_ref, w1_ref, w2_ref, w3_ref, held_ref, sems):
    taps, _, columns_here = couplings_ref.shape
    columns = w1_ref.shape[1]
    blocks = columns // columns_here
    rows_in = 256
    group = rows_in // blocks
    pieces, part = held_ref.shape[0], held_ref.shape[2]
    clusters_here = part // (rank * blocks)

    def piece_copy(i, p):
        return pltpu.make_async_copy(
            couplings_ref.at[p, pl.ds(first * rank * blocks + i * part, part)], held_ref.at[i, p], sems.at[i, p])

    def fetch(i):
        if i < pieces:
            for p in range(taps):
                piece_copy(i, p).start()

    for i in range(depth):
        fetch(i)
    to = lax.broadcasted_iota(jnp.int32, (rows_in, rows_in), 0)
    source = lax.broadcasted_iota(jnp.int32, (rows_in, rows_in), 1)
    wanted = (to % group) * blocks + to // group
    perm = jnp.where(source == wanted, 1.0, 0.0).astype(BF16)

    for i in range(pieces):
        for p in range(taps):
            piece_copy(i, p).wait()
        fetch(i + depth)
        for j in range(clusters_here):
            cluster = i * clusters_here + j
            lag = spread_ref[first + cluster:first + cluster + 1, :]
            masks = []
            for delay in (1.0, 2.0):
                row = jnp.where(lag == delay, 1.0, 0.0)
                masks.append([
                    jnp.broadcast_to(row[:, o * 128:(o + 1) * 128], (group, 128)).astype(BF16)
                    for o in range(blocks)
                ])
            for g in range(rank // group):
                at = j * (rank * blocks) + g * rows_in
                pair = jnp.concatenate([held_ref[i, p, at:at + rows_in, :] for p in range(taps)], axis=1)
                ordered = jnp.dot(perm, pair, preferred_element_type=F32).astype(BF16)
                out = slice(cluster * rank + g * group, cluster * rank + (g + 1) * group)
                for o in range(blocks):
                    k0 = ordered[o * group:(o + 1) * group, :128]
                    k1 = ordered[o * group:(o + 1) * group, 128:]
                    m1, m2 = masks[0][o], masks[1][o]
                    lanes = slice(o * 128, (o + 1) * 128)
                    w1_ref[out, lanes] = k0 * m1
                    w2_ref[out, lanes] = k0 * m2 + k1 * m1
                    w3_ref[out, lanes] = k1 * m2


def build_matrices(first, pieces, couplings, spread, after, depth=3, clusters_here=4):
    sources, columns = spread.shape
    taps, count, width = couplings.shape
    blocks = columns // width
    rank = count // blocks // sources
    matrix = jax.ShapeDtypeStruct((pieces * clusters_here * rank, columns), BF16)
    return pl.pallas_call(
        functools.partial(build_kernel, first, rank, depth),
        out_shape=[matrix] * 3,
        in_specs=[ANY_SPEC, VMEM_SPEC, ANY_SPEC],
        out_specs=[VMEM_SPEC] * 3,
        scratch_shapes=[
            pltpu.VMEM((pieces, taps, clusters_here * rank * blocks, width), BF16),
            pltpu.SemaphoreType.DMA((pieces, taps)),
        ],
        compiler_params=params(20),
        cost_estimate=cost(6 * taps * 256 * matrix.size, 10 * matrix.size),
        name=f"build_matrices{first}",
    )(in_hbm(couplings), spread, after)


def in_hbm(array):
    return pltpu.with_memory_space_constraint(array, pltpu.HBM)


def wide(gathered_ref):
    return jnp.concatenate([gathered_ref[s] for s in range(gathered_ref.shape[0])], axis=1)


def send_field(field_ref, total):
    for o in range(field_ref.shape[0]):
        field_ref[o] = total[:, o * 128:(o + 1) * 128].astype(BF16)


def apply(left, top_ref, bottom_ref):
    half = top_ref.shape[0]
    return (jnp.dot(left[:, :half], top_ref[...], preferred_element_type=F32)
            + jnp.dot(left[:, half:], bottom_ref[...], preferred_element_type=F32))


def step0_kernel(history_ref, transfer_ref, w1a_ref, w1b_ref, w2a_ref, w2b_ref, w3a_ref, w3b_ref,
                 field_ref, base_ref):
    excite = base_ref.shape[1]
    old, middle, new = [
        jnp.concatenate([history_ref[y, x, h] for y in range(4) for x in range(4)], axis=1)
        for h in range(HIST)
    ]
    one = apply(new, w1a_ref, w1b_ref)
    two = apply(jnp.concatenate([middle, new], axis=0), w2a_ref, w2b_ref)
    three = apply(jnp.concatenate([old, middle, new], axis=0), w3a_ref, w3b_ref)
    send_field(field_ref, one + two[:excite] + three[:excite])
    base_ref[0] = two[excite:] + three[excite:2 * excite]
    base_ref[1] = three[2 * excite:]


def step1_kernel(q0_ref, base_ref, w1a_ref, w1b_ref, field_ref):
    send_field(field_ref, base_ref[0] + apply(wide(q0_ref), w1a_ref, w1b_ref))


def step2_kernel(q0_ref, q1_ref, base_ref, w1a_ref, w1b_ref, w2a_ref, w2b_ref, field_ref, next_ref):
    excite = base_ref.shape[1]
    one, zero = wide(q1_ref), wide(q0_ref)
    two = apply(jnp.concatenate([zero, one], axis=0), w2a_ref, w2b_ref)
    send_field(field_ref, base_ref[1] + two[:excite] + apply(one, w1a_ref, w1b_ref))
    next_ref[...] = two[excite:]


def step3_kernel(q0_ref, q1_ref, q2_ref, base_ref, w1a_ref, w1b_ref, w3a_ref, w3b_ref, field_ref, next_ref):
    excite = base_ref.shape[0]
    three = apply(jnp.concatenate([wide(q0_ref), wide(q1_ref)], axis=0), w3a_ref, w3b_ref)
    send_field(field_ref, base_ref[...] + three[:excite] + apply(wide(q2_ref), w1a_ref, w1b_ref))
    next_ref[...] = three[excite:]


def step4_kernel(q2_ref, q3_ref, base_ref, w1a_ref, w1b_ref, w2a_ref, w2b_ref, field_ref):
    send_field(field_ref, base_ref[...] + apply(wide(q2_ref), w2a_ref, w2b_ref)
               + apply(wide(q3_ref), w1a_ref, w1b_ref))


def couple(kernel, name, blocks, extra, gathered, bases, weights):
    excite, width = gathered[0].shape[-2:]
    shapes = [jax.ShapeDtypeStruct((blocks, excite, width), BF16)]
    if extra:
        shapes.append(jax.ShapeDtypeStruct(extra, F32))
    got = pl.pallas_call(
        kernel,
        out_shape=shapes,
        in_specs=[VMEM_SPEC] * (len(gathered) + len(bases) + len(weights)),
        out_specs=[VMEM_SPEC] * len(shapes),
        compiler_params=params(16),
        name=name,
    )(*gathered, *bases, *weights)
    return got if extra else got[0]


def project_kernel(parts_ref, start_ref, transfer_ref, field_ref, out_ref):
    total = parts_ref[0].astype(F32)
    for o in range(1, parts_ref.shape[0]):
        total = total + parts_ref[o].astype(F32)
    field = total.astype(BF16)
    field_ref[...] = field
    q = start_ref[0] - jnp.dot(
        jnp.concatenate([field, field], axis=1), transfer_ref[...], preferred_element_type=F32)
    q = q.astype(BF16)
    for s in range(out_ref.shape[0]):
        out_ref[s] = q


def project_step(parts, start, transfer, copies, step):
    blocks, excite, width = parts.shape
    return pl.pallas_call(
        project_kernel,
        grid=(1,),
        out_shape=(
            jax.ShapeDtypeStruct((excite, width), BF16),
            jax.ShapeDtypeStruct((copies, excite, width), BF16),
        ),
        in_specs=[
            pl.BlockSpec(parts.shape, lambda i: (0, 0, 0)),
            pl.BlockSpec((1, excite, width), lambda i: (step, 0, 0)),
            pl.BlockSpec(transfer.shape, lambda i: (0, 0)),
        ],
        out_specs=(
            pl.BlockSpec((excite, width), lambda i: (0, 0)),
            pl.BlockSpec((copies, excite, width), lambda i: (0, 0, 0)),
        ),
        compiler_params=params(8),
        name="project_step",
    )(parts, start, transfer)


def summed(parts_ref):
    total = parts_ref[0].astype(F32)
    for o in range(1, parts_ref.shape[0]):
        total = total + parts_ref[o].astype(F32)
    return total.astype(BF16)


def currents_kernel(incoming_ref, expanded_ref, parts_ref, f0_ref, f1_ref, f2_ref, f3_ref, out_ref, made_ref, sems):
    fields = [f0_ref[...], f1_ref[...], f2_ref[...], f3_ref[...], summed(parts_ref)]
    steps, clusters, excite, unknowns = made_ref.shape
    rank = expanded_ref.shape[1]
    copies = []
    for c in range(clusters):
        for first, last in ((0, steps // 2), (steps // 2, steps)):
            left = jnp.concatenate([f[:, c * rank:(c + 1) * rank] for f in fields[first:last]], axis=0)
            far = jnp.dot(left, expanded_ref[c], preferred_element_type=F32)
            for t in range(first, last):
                own = far[(t - first) * excite:(t - first + 1) * excite]
                made_ref[t, c] = (incoming_ref[t, c].astype(F32) - own).astype(BF16)
                copy = pltpu.make_async_copy(made_ref.at[t, c], out_ref.at[t, c], sems.at[t, c])
                copy.start()
                copies.append(copy)
    for copy in copies:
        copy.wait()


def final_currents(incoming, expanded, parts, fields):
    return pl.pallas_call(
        currents_kernel,
        out_shape=jax.ShapeDtypeStruct(incoming.shape, BF16),
        in_specs=[VMEM_SPEC] * (3 + len(fields)),
        out_specs=ANY_SPEC,
        scratch_shapes=[
            pltpu.VMEM(incoming.shape, BF16),
            pltpu.SemaphoreType.DMA(incoming.shape[:2]),
        ],
        compiler_params=params(12),
        name="final_currents",
    )(incoming, expanded, parts, *fields)


def per_device(history, incident, proj_basis, expand_basis, near_inverse, couplings, lags):
    clusters, rank, unknowns = proj_basis.shape
    width = clusters * rank
    taps, src_rows, blocks = couplings.shape[:3]
    pairs = lags.transpose(1, 2, 3, 0)[:, 0]
    senders = src_rows // width
    flat = couplings.reshape(taps, src_rows * blocks, width)
    def gather(copies):
        return lax.all_to_all(copies, "src", 0, 0)

    def scatter(chunks):
        return lax.all_to_all(chunks, "obs", 0, 0)

    mine, spread = project_history(history, proj_basis, pairs)
    arrived = swap(mine, 1)
    top = build_matrices(0, TOP, flat, spread, mine)
    mine = ordered(mine, arrived, top[0], 1, "order_x")
    arrived = swap(mine, 4)
    bottom = build_matrices(4 * TOP, 8 - TOP, flat, spread, mine)
    incoming, expanded, start, transfer = prepare_near(incident, expand_basis, near_inverse, proj_basis, bottom[0])
    w1, w2, w3 = [list(halves) for halves in zip(top, bottom)]
    gathered = ordered(mine, arrived, transfer, 4, "order_y")
    fields, past = [], []
    excite = history.shape[2]
    full = (excite, blocks * width)
    ahead = None
    for step in range(STEPS):
        if step == 0:
            chunks, base = couple(step0_kernel, "step0", blocks, (2,) + full, [gathered], [transfer], w1 + w2 + w3)
        elif step == 1:
            chunks = couple(step1_kernel, "step1", blocks, None, past, [base], w1)
        elif step == 2:
            chunks, ahead = couple(step2_kernel, "step2", blocks, full, past, [base], w1 + w2)
        elif step == 3:
            chunks, ahead = couple(step3_kernel, "step3", blocks, full, past, [ahead], w1 + w3)
        else:
            chunks = couple(step4_kernel, "step4", blocks, None, past[2:], [ahead], w1 + w2)
        parts = scatter(chunks)
        if step + 1 < STEPS:
            field, copies = project_step(parts, start, transfer, senders, step)
            fields.append(field)
            past.append(gather(copies))
    return final_currents(incoming, expanded, parts, fields)


def solution(mesh):
    placed = (
        P(None, ("obs", "src"), None, None),
        P(None, ("obs", "src"), None, None),
        P(("obs", "src"), None, None),
        P(("obs", "src"), None, None),
        P(("obs", "src"), None, None),
        P(None, "obs", None, "src", None),
        P("obs", None, "src", None),
    )
    return jax.shard_map(
        per_device,
        mesh=mesh,
        in_specs=placed,
        out_specs=P(None, ("obs", "src"), None, None),
        check_vma=False,
    )
```

```python
import functools

import jax
import jax.numpy as jnp
from jax import lax
from jax.experimental import pallas as pl
from jax.experimental.pallas import tpu as pltpu
from jax.sharding import PartitionSpec as P

STEPS = 5
HIST = 3
TOP = 5
MIB = 1024 * 1024
BF16 = jnp.bfloat16
F32 = jnp.float32
ANY_SPEC = pl.BlockSpec(memory_space=pl.ANY)
VMEM_SPEC = pl.BlockSpec(memory_space=pltpu.VMEM)


def nt_dot(left, right):
    return lax.dot_general(left, right, (((1,), (1,)), ((), ())), preferred_element_type=F32)


def params(limit, **more):
    return pltpu.CompilerParams(vmem_limit_bytes=limit * MIB, **more)


def cost(flops, touched):
    return pl.CostEstimate(flops=int(flops), bytes_accessed=int(touched), transcendentals=0)


def history_kernel(history_ref, proj_ref, lags_ref, out_ref, spread_ref, held_ref, basis_ref, pairs_ref, sems, pairs_sem):
    slots, clusters, excite, unknowns = held_ref.shape
    blocks, observers, sources = lags_ref.shape
    columns = spread_ref.shape[1]
    pairs_copy = pltpu.make_async_copy(lags_ref, pairs_ref, pairs_sem)
    pairs_copy.start()
    copies = []
    for c in range(clusters):
        copies.append((
            pltpu.make_async_copy(proj_ref.at[c], basis_ref.at[c], sems.at[c, slots]),
            [pltpu.make_async_copy(history_ref.at[h, c], held_ref.at[h, c], sems.at[c, h]) for h in range(slots)],
        ))
    for basis, parts in copies:
        for part in parts:
            part.start()
        basis.start()
    pairs_copy.wait()
    pairs = jnp.concatenate([pairs_ref[o] for o in range(blocks)], axis=0).astype(F32)
    owner = lax.broadcasted_iota(jnp.int32, (blocks * observers, columns), 1) // (columns // (blocks * observers))
    row = lax.broadcasted_iota(jnp.int32, (blocks * observers, columns), 0)
    spread_ref[...] = lax.dot_general(
        pairs, jnp.where(owner == row, 1.0, 0.0), (((0,), (0,)), ((), ())), preferred_element_type=F32)
    sides = []
    for c, (basis, parts) in enumerate(copies):
        for part in parts:
            part.wait()
        basis.wait()
        left = jnp.concatenate([held_ref[h, c] for h in range(slots)], axis=0)
        sides.append(nt_dot(left, basis_ref[c]))
    both = jnp.concatenate(sides, axis=1).astype(BF16)
    for h in range(slots):
        out_ref[h] = both[h * excite:(h + 1) * excite]


def project_history(history, proj_basis, lags):
    slots, clusters, excite, unknowns = history.shape
    rank = proj_basis.shape[1]
    blocks, observers, sources = lags.shape
    return pl.pallas_call(
        history_kernel,
        out_shape=(
            jax.ShapeDtypeStruct((slots, excite, clusters * rank), BF16),
            jax.ShapeDtypeStruct((sources, blocks * observers * rank), F32),
        ),
        in_specs=[ANY_SPEC] * 3,
        out_specs=[VMEM_SPEC] * 2,
        scratch_shapes=[
            pltpu.VMEM(history.shape, BF16),
            pltpu.VMEM(proj_basis.shape, BF16),
            pltpu.VMEM(lags.shape, lags.dtype),
            pltpu.SemaphoreType.DMA((clusters, slots + 1)),
            pltpu.SemaphoreType.DMA,
        ],
        compiler_params=params(8),
        name="project_history",
    )(in_hbm(history), in_hbm(proj_basis), in_hbm(lags))


def order_kernel(stride, own_ref, by1_ref, by3_ref, by2_ref, after_ref, out_ref):
    me = lax.rem(lax.axis_index("src") // stride, 4)
    for k, ref in ((0, own_ref), (1, by1_ref), (3, by3_ref), (2, by2_ref)):
        out_ref[me ^ k] = ref[...]


def swap(array, stride):
    return [lax.ppermute(array, "src", [(i, i ^ (k * stride)) for i in range(16)]) for k in (1, 3, 2)]


def ordered(array, arrived, after, stride, name):
    return pl.pallas_call(
        functools.partial(order_kernel, stride),
        out_shape=jax.ShapeDtypeStruct((4,) + array.shape, array.dtype),
        in_specs=[VMEM_SPEC] * 4 + [ANY_SPEC],
        out_specs=VMEM_SPEC,
        compiler_params=params(8),
        name=name,
    )(array, *arrived, after)


def near_kernel(tile, incident_ref, expand_ref, near_ref, proj_ref, after_ref,
                incoming_ref, expanded_ref, start_ref, transfer_ref):
    steps, clusters, excite, unknowns = incident_ref.shape
    rank = expand_ref.shape[1]
    head = steps * excite
    small = []
    for c in range(clusters):
        left = jnp.concatenate([incident_ref[t, c] for t in range(steps)] + [expand_ref[c]], axis=0)
        total = None
        for n in range(unknowns // tile):
            lanes = slice(n * tile, (n + 1) * tile)
            product = jnp.dot(left, near_ref[c, :, lanes], preferred_element_type=F32).astype(BF16)
            for t in range(steps):
                incoming_ref[t, c, :, lanes] = product[t * excite:(t + 1) * excite]
            expanded_ref[c, :, lanes] = product[head:]
            part = nt_dot(product, proj_ref[c, :, lanes])
            total = part if total is None else total + part
        small.append(total)
    for t in range(steps):
        rows = slice(t * excite, (t + 1) * excite)
        start_ref[t] = jnp.concatenate([part[rows] for part in small], axis=1)
    zero = jnp.zeros((rank, rank), F32)
    full = jnp.concatenate([
        jnp.concatenate([small[0][head:], zero], axis=1),
        jnp.concatenate([zero, small[1][head:]], axis=1),
    ], axis=0)
    high = full.astype(BF16)
    low = (full - high.astype(F32)).astype(BF16)
    transfer_ref[...] = jnp.concatenate([high, low], axis=0)


def prepare_near(incident, expand_basis, near_inverse, proj_basis, after, tile=512):
    steps, clusters, excite, unknowns = incident.shape
    rank = proj_basis.shape[1]
    rows = steps * excite + rank
    return pl.pallas_call(
        functools.partial(near_kernel, tile),
        out_shape=(
            jax.ShapeDtypeStruct((steps, clusters, excite, unknowns), BF16),
            jax.ShapeDtypeStruct((clusters, rank, unknowns), BF16),
            jax.ShapeDtypeStruct((steps, excite, clusters * rank), F32),
            jax.ShapeDtypeStruct((2 * clusters * rank, clusters * rank), BF16),
        ),
        in_specs=[VMEM_SPEC] * 4 + [ANY_SPEC],
        out_specs=[VMEM_SPEC] * 4,
        compiler_params=params(20),
        cost_estimate=cost(2 * clusters * rows * unknowns * (unknowns + rank), 2 * clusters * unknowns * unknowns),
        name="prepare_near",
    )(incident, expand_basis, near_inverse, proj_basis, after)


def build_kernel(first, rank, depth, couplings_ref, spread_ref, after_ref, w1_ref, w2_ref, w3_ref, held_ref, sems):
    taps, _, columns_here = couplings_ref.shape
    columns = w1_ref.shape[1]
    blocks = columns // columns_here
    rows_in = 256
    group = rows_in // blocks
    pieces, part = held_ref.shape[0], held_ref.shape[2]
    clusters_here = part // (rank * blocks)

    def piece_copy(i, p):
        return pltpu.make_async_copy(
            couplings_ref.at[p, pl.ds(first * rank * blocks + i * part, part)], held_ref.at[i, p], sems.at[i, p])

    def fetch(i):
        if i < pieces:
            for p in range(taps):
                piece_copy(i, p).start()

    for i in range(depth):
        fetch(i)
    to = lax.broadcasted_iota(jnp.int32, (rows_in, rows_in), 0)
    source = lax.broadcasted_iota(jnp.int32, (rows_in, rows_in), 1)
    wanted = (to % group) * blocks + to // group
    perm = jnp.where(source == wanted, 1.0, 0.0).astype(BF16)

    for i in range(pieces):
        for p in range(taps):
            piece_copy(i, p).wait()
        fetch(i + depth)
        for j in range(clusters_here):
            cluster = i * clusters_here + j
            lag = spread_ref[first + cluster:first + cluster + 1, :]
            masks = []
            for delay in (1.0, 2.0):
                row = jnp.where(lag == delay, 1.0, 0.0)
                masks.append([
                    jnp.broadcast_to(row[:, o * 128:(o + 1) * 128], (group, 128)).astype(BF16)
                    for o in range(blocks)
                ])
            for g in range(rank // group):
                at = j * (rank * blocks) + g * rows_in
                pair = jnp.concatenate([held_ref[i, p, at:at + rows_in, :] for p in range(taps)], axis=1)
                ordered = jnp.dot(perm, pair, preferred_element_type=F32).astype(BF16)
                out = slice(cluster * rank + g * group, cluster * rank + (g + 1) * group)
                for o in range(blocks):
                    k0 = ordered[o * group:(o + 1) * group, :128]
                    k1 = ordered[o * group:(o + 1) * group, 128:]
                    m1, m2 = masks[0][o], masks[1][o]
                    lanes = slice(o * 128, (o + 1) * 128)
                    w1_ref[out, lanes] = k0 * m1
                    w2_ref[out, lanes] = k0 * m2 + k1 * m1
                    w3_ref[out, lanes] = k1 * m2


def build_matrices(first, pieces, couplings, spread, after, depth=5, clusters_here=4):
    sources, columns = spread.shape
    taps, count, width = couplings.shape
    blocks = columns // width
    rank = count // blocks // sources
    matrix = jax.ShapeDtypeStruct((pieces * clusters_here * rank, columns), BF16)
    return pl.pallas_call(
        functools.partial(build_kernel, first, rank, depth),
        out_shape=[matrix] * 3,
        in_specs=[ANY_SPEC, VMEM_SPEC, ANY_SPEC],
        out_specs=[VMEM_SPEC] * 3,
        scratch_shapes=[
            pltpu.VMEM((pieces, taps, clusters_here * rank * blocks, width), BF16),
            pltpu.SemaphoreType.DMA((pieces, taps)),
        ],
        compiler_params=params(20),
        cost_estimate=cost(6 * taps * 256 * matrix.size, 10 * matrix.size),
        name=f"build_matrices{first}",
    )(in_hbm(couplings), spread, after)


def in_hbm(array):
    return pltpu.with_memory_space_constraint(array, pltpu.HBM)


def wide(gathered_ref):
    return jnp.concatenate([gathered_ref[s] for s in range(gathered_ref.shape[0])], axis=1)


def send_field(field_ref, total):
    for o in range(field_ref.shape[0]):
        field_ref[o] = total[:, o * 128:(o + 1) * 128].astype(BF16)


def apply(left, top_ref, bottom_ref):
    half = top_ref.shape[0]
    return (jnp.dot(left[:, :half], top_ref[...], preferred_element_type=F32)
            + jnp.dot(left[:, half:], bottom_ref[...], preferred_element_type=F32))


def step0_kernel(history_ref, transfer_ref, w1a_ref, w1b_ref, w2a_ref, w2b_ref, w3a_ref, w3b_ref,
                 field_ref, base_ref):
    excite = base_ref.shape[1]
    old, middle, new = [
        jnp.concatenate([history_ref[y, x, h] for y in range(4) for x in range(4)], axis=1)
        for h in range(HIST)
    ]
    one = apply(new, w1a_ref, w1b_ref)
    two = apply(jnp.concatenate([middle, new], axis=0), w2a_ref, w2b_ref)
    three = apply(jnp.concatenate([old, middle, new], axis=0), w3a_ref, w3b_ref)
    send_field(field_ref, one + two[:excite] + three[:excite])
    base_ref[0] = two[excite:] + three[excite:2 * excite]
    base_ref[1] = three[2 * excite:]


def step1_kernel(q0_ref, base_ref, w1a_ref, w1b_ref, field_ref):
    send_field(field_ref, base_ref[0] + apply(wide(q0_ref), w1a_ref, w1b_ref))


def step2_kernel(q0_ref, q1_ref, base_ref, w1a_ref, w1b_ref, w2a_ref, w2b_ref, field_ref, next_ref):
    excite = base_ref.shape[1]
    one, zero = wide(q1_ref), wide(q0_ref)
    two = apply(jnp.concatenate([zero, one], axis=0), w2a_ref, w2b_ref)
    send_field(field_ref, base_ref[1] + two[:excite] + apply(one, w1a_ref, w1b_ref))
    next_ref[...] = two[excite:]


def step3_kernel(q0_ref, q1_ref, q2_ref, base_ref, w1a_ref, w1b_ref, w3a_ref, w3b_ref, field_ref, next_ref):
    excite = base_ref.shape[0]
    three = apply(jnp.concatenate([wide(q0_ref), wide(q1_ref)], axis=0), w3a_ref, w3b_ref)
    send_field(field_ref, base_ref[...] + three[:excite] + apply(wide(q2_ref), w1a_ref, w1b_ref))
    next_ref[...] = three[excite:]


def step4_kernel(q2_ref, q3_ref, base_ref, w1a_ref, w1b_ref, w2a_ref, w2b_ref, field_ref):
    send_field(field_ref, base_ref[...] + apply(wide(q2_ref), w2a_ref, w2b_ref)
               + apply(wide(q3_ref), w1a_ref, w1b_ref))


def couple(kernel, name, blocks, extra, gathered, bases, weights):
    excite, width = gathered[0].shape[-2:]
    shapes = [jax.ShapeDtypeStruct((blocks, excite, width), BF16)]
    if extra:
        shapes.append(jax.ShapeDtypeStruct(extra, F32))
    got = pl.pallas_call(
        kernel,
        out_shape=shapes,
        in_specs=[VMEM_SPEC] * (len(gathered) + len(bases) + len(weights)),
        out_specs=[VMEM_SPEC] * len(shapes),
        compiler_params=params(16),
        name=name,
    )(*gathered, *bases, *weights)
    return got if extra else got[0]


def project_kernel(parts_ref, start_ref, transfer_ref, field_ref, out_ref):
    total = parts_ref[0].astype(F32)
    for o in range(1, parts_ref.shape[0]):
        total = total + parts_ref[o].astype(F32)
    field = total.astype(BF16)
    field_ref[...] = field
    q = start_ref[0] - jnp.dot(
        jnp.concatenate([field, field], axis=1), transfer_ref[...], preferred_element_type=F32)
    q = q.astype(BF16)
    for s in range(out_ref.shape[0]):
        out_ref[s] = q


def project_step(parts, start, transfer, copies, step):
    blocks, excite, width = parts.shape
    return pl.pallas_call(
        project_kernel,
        grid=(1,),
        out_shape=(
            jax.ShapeDtypeStruct((excite, width), BF16),
            jax.ShapeDtypeStruct((copies, excite, width), BF16),
        ),
        in_specs=[
            pl.BlockSpec(parts.shape, lambda i: (0, 0, 0)),
            pl.BlockSpec((1, excite, width), lambda i: (step, 0, 0)),
            pl.BlockSpec(transfer.shape, lambda i: (0, 0)),
        ],
        out_specs=(
            pl.BlockSpec((excite, width), lambda i: (0, 0)),
            pl.BlockSpec((copies, excite, width), lambda i: (0, 0, 0)),
        ),
        compiler_params=params(8),
        name="project_step",
    )(parts, start, transfer)


def summed(parts_ref):
    total = parts_ref[0].astype(F32)
    for o in range(1, parts_ref.shape[0]):
        total = total + parts_ref[o].astype(F32)
    return total.astype(BF16)


def currents_kernel(incoming_ref, expanded_ref, parts_ref, f0_ref, f1_ref, f2_ref, f3_ref, out_ref, made_ref, sems):
    fields = [f0_ref[...], f1_ref[...], f2_ref[...], f3_ref[...], summed(parts_ref)]
    steps, clusters, excite, unknowns = made_ref.shape
    rank = expanded_ref.shape[1]
    copies = []
    for c in range(clusters):
        for first, last in ((0, steps // 2), (steps // 2, steps)):
            left = jnp.concatenate([f[:, c * rank:(c + 1) * rank] for f in fields[first:last]], axis=0)
            far = jnp.dot(left, expanded_ref[c], preferred_element_type=F32)
            for t in range(first, last):
                own = far[(t - first) * excite:(t - first + 1) * excite]
                made_ref[t, c] = (incoming_ref[t, c].astype(F32) - own).astype(BF16)
                copy = pltpu.make_async_copy(made_ref.at[t, c], out_ref.at[t, c], sems.at[t, c])
                copy.start()
                copies.append(copy)
    for copy in copies:
        copy.wait()


def final_currents(incoming, expanded, parts, fields):
    return pl.pallas_call(
        currents_kernel,
        out_shape=jax.ShapeDtypeStruct(incoming.shape, BF16),
        in_specs=[VMEM_SPEC] * (3 + len(fields)),
        out_specs=ANY_SPEC,
        scratch_shapes=[
            pltpu.VMEM(incoming.shape, BF16),
            pltpu.SemaphoreType.DMA(incoming.shape[:2]),
        ],
        compiler_params=params(12),
        name="final_currents",
    )(incoming, expanded, parts, *fields)


def per_device(history, incident, proj_basis, expand_basis, near_inverse, couplings, lags):
    clusters, rank, unknowns = proj_basis.shape
    width = clusters * rank
    taps, src_rows, blocks = couplings.shape[:3]
    pairs = lags.transpose(1, 2, 3, 0)[:, 0]
    senders = src_rows // width
    flat = couplings.reshape(taps, src_rows * blocks, width)
    def gather(copies):
        return lax.all_to_all(copies, "src", 0, 0)

    def scatter(chunks):
        return lax.all_to_all(chunks, "obs", 0, 0)

    mine, spread = project_history(history, proj_basis, pairs)
    arrived = swap(mine, 1)
    top = build_matrices(0, TOP, flat, spread, mine)
    mine = ordered(mine, arrived, top[0], 1, "order_x")
    arrived = swap(mine, 4)
    bottom = build_matrices(4 * TOP, 8 - TOP, flat, spread, mine)
    incoming, expanded, start, transfer = prepare_near(incident, expand_basis, near_inverse, proj_basis, bottom[0])
    w1, w2, w3 = [list(halves) for halves in zip(top, bottom)]
    gathered = ordered(mine, arrived, transfer, 4, "order_y")
    fields, past = [], []
    excite = history.shape[2]
    full = (excite, blocks * width)
    ahead = None
    for step in range(STEPS):
        if step == 0:
            chunks, base = couple(step0_kernel, "step0", blocks, (2,) + full, [gathered], [transfer], w1 + w2 + w3)
        elif step == 1:
            chunks = couple(step1_kernel, "step1", blocks, None, past, [base], w1)
        elif step == 2:
            chunks, ahead = couple(step2_kernel, "step2", blocks, full, past, [base], w1 + w2)
        elif step == 3:
            chunks, ahead = couple(step3_kernel, "step3", blocks, full, past, [ahead], w1 + w3)
        else:
            chunks = couple(step4_kernel, "step4", blocks, None, past[2:], [ahead], w1 + w2)
        parts = scatter(chunks)
        if step + 1 < STEPS:
            field, copies = project_step(parts, start, transfer, senders, step)
            fields.append(field)
            past.append(gather(copies))
    return final_currents(incoming, expanded, parts, fields)


def solution(mesh):
    placed = (
        P(None, ("obs", "src"), None, None),
        P(None, ("obs", "src"), None, None),
        P(("obs", "src"), None, None),
        P(("obs", "src"), None, None),
        P(("obs", "src"), None, None),
        P(None, "obs", None, "src", None),
        P("obs", None, "src", None),
    )
    return jax.shard_map(
        per_device,
        mesh=mesh,
        in_specs=placed,
        out_specs=P(None, ("obs", "src"), None, None),
        check_vma=False,
    )
```
